128 devices in a mesh: trow: 8 (over z, y_lo), tcol: 16 (over x, y_hi, core).
Axes of the slice: x: 4, y: 4 (y_hi: 2, y_lo: 2; y = y_hi * 2 + y_lo), z: 4, core: 2. Of those that a mesh axis runs over, the one named last changes fastest.
Arguments:
- gaussian: bfloat16 [98304, 512], P('trow', 'tcol'), may hold values from -6 to 6
- left_basis: bfloat16 [48, 48, 2048, 128], P('tcol', 'trow'), may hold values from -0.109375 to 0.109375
- right_basis: bfloat16 [48, 48, 2048, 128], P('tcol', 'trow'), may hold values from -0.125 to 0.125
- tile_ranks: int32 [48, 48], P('tcol', 'trow'), may hold values from 0 to 128, as said below
- diag_factor: bfloat16 [48, 2048, 2048], P('tcol', 'trow')
- morton_of_grid: int32 [98304], P('tcol'), may hold values from 0 to 98303, as said below
Outputs:
- grid_fields: bfloat16 [98304, 512], P('tcol', 'trow')
The draws below stay inside these ranges and needn't reach their ends.
Inputs may be any that keep to these rules, and one draw needn't show every extreme that they name: `tile_ranks`: in tile order, zero unless the tile row lies below the tile column; below it from 16 to 128, both reached. `morton_of_grid`: a permutation; for every g below 16, each block of 6144 consecutive entries holds exactly 384 Morton indices whose tile (index div 2048) is g modulo 16.
All inputs are finite; a program needn't handle non-finite values.
Results may differ from the reference program's by a relative error of at most 0.0032.
Values may be sent and summed in bfloat16 or wider, within the bound.
A program may use at most 192 MiB of HBM per device.

```python
import jax
import jax.numpy as jnp
from jax import lax

TILE = 2048
RANK = 128
FIELDS = 512
TR_DEV = 3
NT = 48
TC_DEV = 6
POINTS = 98304
RGROUPS = 16
CGROUPS = 8
PTS_DEV = 6144
SLOT = 384


def draw_tile_ranks(key, part):
    key = jax.random.fold_in(key, 11)
    values = jax.random.randint(key, (NT, NT), RANK // 8, RANK + 1)
    stored = jnp.arange(NT, dtype=jnp.int32)
    row_tiles = (stored % TR_DEV * RGROUPS + stored // TR_DEV)[:, None]
    col_tiles = (stored % TC_DEV * CGROUPS + stored // TC_DEV)[None, :]
    values = jnp.where(row_tiles > col_tiles, values, 0)
    last_row = (NT - 1) % RGROUPS * TR_DEV + (NT - 1) // RGROUPS
    second_row = 1 % RGROUPS * TR_DEV + 1 // RGROUPS
    values = values.at[last_row, 0].set(RANK // 8)
    values = values.at[second_row, 0].set(RANK)
    return values.astype(jnp.int32)


def draw_diag_factor(key, part):
    key = jax.random.fold_in(key, 23)
    key_lower, key_diag = jax.random.split(key)
    lower_part = jax.random.normal(key_lower, (NT, TILE, TILE), jnp.float32)
    lower_part = lower_part * TILE ** (-0.5)
    row_index = jnp.arange(TILE, dtype=jnp.int32)[:, None]
    col_index = jnp.arange(TILE, dtype=jnp.int32)[None, :]
    lower_part = jnp.where(row_index > col_index, lower_part, 0.0)
    middle = jax.random.uniform(key_diag, (NT, TILE), jnp.float32, 0.5, 1.5)
    lower_part = lower_part + jnp.where(row_index == col_index, 1.0, 0.0)[None] * middle[:, :, None]
    return lower_part.astype(jnp.bfloat16)


def draw_morton_of_grid(key, part):
    key = jax.random.fold_in(key, 37)
    key_split, key_order = jax.random.split(key)
    split_keys = jax.random.split(key_split, RGROUPS)
    local_rows = jax.vmap(lambda one_key: jax.random.permutation(one_key, PTS_DEV))(split_keys).astype(jnp.int32)
    local_rows = local_rows.reshape(RGROUPS, RGROUPS, SLOT).transpose(1, 0, 2)
    source_group = jnp.arange(RGROUPS, dtype=jnp.int32)[None, :, None]
    tile_index = local_rows // TILE * RGROUPS + source_group
    morton = (tile_index * TILE + local_rows % TILE).reshape(RGROUPS, PTS_DEV)
    order_keys = jax.random.split(key_order, RGROUPS)
    orders = jax.vmap(lambda one_key: jax.random.permutation(one_key, PTS_DEV))(order_keys).astype(jnp.int32)
    morton = jnp.take_along_axis(morton, orders, axis=1)
    return morton.reshape(POINTS).astype(jnp.int32)


def steps_of(rng, shape, shards, least, largest):
    def one(axis_at, shards_of):
        steps = jax.random.uniform(jax.random.fold_in(jax.random.fold_in(rng, 6), axis_at), (shards_of,), jnp.float32, least / len(shards), largest / len(shards))
        return jnp.repeat(jnp.exp(steps), shape[axis_at] // shards_of).reshape((-1,) + (1,) * (len(shape) - axis_at - 1))

    gain = one(*shards[0])
    for cut in shards[1:]:
        gain = gain * one(*cut)
    return gain


def scatter_about(own_key, extent, width, limit, cuts=(), kind=jnp.bfloat16):
    array = width * jax.random.normal(own_key, extent, jnp.float32)
    if cuts:
        array = array * steps_of(own_key, extent, cuts, -0.22, 0.18)
    return jnp.clip(array, -limit, limit).astype(kind)


def setup_inputs(seed: int = 0) -> dict:
    splits = jax.random.split(jax.random.key(seed), 7)
    gaussian = scatter_about(splits[0], (POINTS, FIELDS), 1.0, 6.0, ((0, 8), (1, 16)))
    left_basis = scatter_about(splits[1], (NT, NT, TILE, RANK), (RANK * NT // 2) ** -0.5, 0.109375, ((0, 16), (1, 8)))
    right_basis = scatter_about(splits[2], (NT, NT, TILE, RANK), TILE ** -0.5, 0.125, ((0, 16), (1, 8)))
    tile_ranks = draw_tile_ranks(jax.random.fold_in(splits[6], 71), 0)
    diag_factor = draw_diag_factor(jax.random.fold_in(splits[6], 71), 0)
    morton_of_grid = draw_morton_of_grid(jax.random.fold_in(splits[6], 71), 0)
    return dict(gaussian=gaussian, left_basis=left_basis, right_basis=right_basis, tile_ranks=tile_ranks, diag_factor=diag_factor, morton_of_grid=morton_of_grid)


def reference(gaussian, left_basis, right_basis, tile_ranks, diag_factor, morton_of_grid):
    blocks_all = gaussian.reshape(NT, TILE, FIELDS)
    kept_rows = jnp.arange(RANK, dtype=jnp.int32)[None, None, :] < tile_ranks[:, :, None]
    stored = jnp.arange(NT, dtype=jnp.int32)
    row_tile_of = (stored % TR_DEV) * RGROUPS + stored // TR_DEV
    col_stored_of = (stored % CGROUPS) * TC_DEV + stored // CGROUPS
    row_stored_of = (stored % RGROUPS) * TR_DEV + stored // RGROUPS

    def tile_row(stored_row):
        right_rows = right_basis[stored_row].astype(jnp.float32)
        left_rows = left_basis[stored_row].astype(jnp.float32)
        coeffs = jnp.einsum('jbr,jbs->jrs', right_rows, blocks_all.astype(jnp.float32))
        coeffs = jnp.where(kept_rows[stored_row][:, :, None], coeffs, 0.0).astype(jnp.bfloat16)
        lowrank = jnp.einsum('jbr,jrs->bs', left_rows, coeffs.astype(jnp.float32))
        diag_col = col_stored_of[row_tile_of[stored_row]]
        diag_block = lax.dynamic_index_in_dim(blocks_all, diag_col, 0, keepdims=False)
        diag_term = jnp.dot(diag_factor[stored_row], diag_block, preferred_element_type=jnp.float32)
        return lowrank + diag_term

    results = lax.map(tile_row, stored)
    morton_fields = jnp.take(results, row_stored_of, axis=0)
    morton_fields = morton_fields.reshape(POINTS, FIELDS).astype(jnp.bfloat16)
    return jnp.take(morton_fields, morton_of_grid, axis=0)
```

```python
import jax
import jax.numpy as jnp
from jax import lax
from jax.experimental import pallas as pl
from jax.experimental.pallas import tpu as pltpu
from jax.sharding import PartitionSpec as P

MESH = pl.DeviceIdType.MESH
F32 = jnp.float32
BF16 = jnp.bfloat16
TILE = 2048
RANK = 128
FIELDS = 512
NK = 3
GC = 16
GT = 8
MINE = FIELDS // GC
OUTF = FIELDS // GT
CHUNK = 2 * TILE
BAND = TILE // GT
PTS = NK * TILE
SLOT = PTS // GC


def place():
    t = lax.axis_index("trow")
    c = lax.axis_index("tcol")
    return t, c


def sums_kernel(
    zt, left, right, ranks, diag, wanted,
    out, asked,
    zf, pt, b0, b1, b2, a0, a1, a2, r0, r1, r2, snd, rcv,
    g_send, g_recv, d_send, d_recv, z_send, z_recv, s_send, s_recv, l_send, l_recv, loc_r, loc_b, loc_z, loc_d, loc_l,
):
    t, c = place()
    z, yl = t // 2, t % 2
    x, yh, core = c // 4, (c // 2) % 2, c % 2
    bs = (b0, b1, b2)
    as_ = (a0, a1, a2)
    rs = (r0, r1, r2)

    def cat(xx, yy, cc):
        return lax.rem(xx + 4, 4) * 4 + yy * 2 + cc

    def tat(zz, yy):
        return lax.rem(zz + 4, 4) * 2 + yy

    own_root = (c % GT) == t

    barrier = pltpu.get_barrier_semaphore()
    for d in range(1, GT):
        pl.semaphore_signal(barrier, inc=1, device_id=(lax.rem(t + d, GT), c), device_id_type=MESH)
    for d in range(1, GC):
        pl.semaphore_signal(barrier, inc=1, device_id=(t, lax.rem(c + d, GC)), device_id_type=MESH)
    for d in range(1, GC):
        pl.semaphore_signal(barrier, inc=1, device_id=(c % GT, lax.rem(c + d, GC)), device_id_type=MESH)

    @pl.when(jnp.logical_not(own_root))
    def _():
        pl.semaphore_signal(barrier, inc=1, device_id=(c % GT, c), device_id_type=MESH)

    pl.semaphore_wait(barrier, GT - 1 + GC - 1 + GC - jnp.where(own_root, 1, 0))

    def block(k, cc):
        return zf.at[k, pl.ds(pl.multiple_of(cc * MINE, MINE), MINE), :]

    def remote(src, dst, ssem, rsem, dev):
        return pltpu.make_async_remote_copy(
            src_ref=src, dst_ref=dst, send_sem=ssem, recv_sem=rsem, device_id=dev, device_id_type=MESH)

    sent = []

    def go(cp):
        cp.start()
        sent.append(cp)

    xp = (t, cat(x + 1, yh, core))
    xm = (t, cat(x - 1, yh, core))
    yp = (t, cat(x, 1 - yh, core))
    sib = (t, cat(x, yh, 1 - core))
    zp = (tat(z + 1, yl), c)
    zm = (tat(z - 1, yl), c)
    ylp = (tat(z, 1 - yl), c)

    def slot_block(i, cc):
        return (
            cat(x, 1 - yh, cc), cat(x - 1, yh, cc), cat(x + 1, yh, cc), cat(x - 1, 1 - yh, cc),
            cat(x + 1, 1 - yh, cc), cat(x - 2, yh, cc), cat(x + 2, 1 - yh, cc))[i]

    def fwd(k, i_block, src, i_send, slot, dev):
        go(remote(src, block(k, i_block), g_send.at[k, i_send], g_recv.at[k, slot], dev))

    def got(k, slot, cc):
        ref = block(k, cc)
        pltpu.make_async_copy(ref, ref, g_recv.at[k, slot]).wait()

    def gather_a(k):
        src = zt.at[:, pl.ds(k * CHUNK, CHUNK)]
        fwd(k, c, src, 0, 0, yp)
        fwd(k, c, src, 1, 1, xp)
        fwd(k, c, src, 2, 2, xm)
        fwd(k, c, src, 7, 7, sib)

    def relay(k, i, targets):
        cc = slot_block(i, core)
        got(k, i, cc)
        for i_send, slot, dev in targets:
            fwd(k, cc, block(k, cc), i_send, slot, dev)
        fwd(k, cc, block(k, cc), 8 + i, 8 + i, sib)

    def gather_b(k):
        relay(k, 0, ((3, 3, xp), (4, 4, xm)))
        relay(k, 1, ((5, 5, xp),))
        relay(k, 2, ())

    def gather_c(k):
        relay(k, 3, ())
        relay(k, 4, ((6, 6, xm),))
        relay(k, 5, ())
        relay(k, 6, ())

    def gather_d(k):
        got(k, 7, cat(x, yh, 1 - core))
        for i in range(7):
            got(k, 8 + i, slot_block(i, 1 - core))

    def diag_cols(k, tt):
        return diag.at[k, :, pl.ds(pl.multiple_of(tt * BAND, BAND), BAND)]

    def diag_rows(k, tt):
        return bs[k].at[pl.ds(pl.multiple_of(tt * BAND, BAND), BAND), pl.ds((k + 1) * 2 * RANK, BAND)]

    def diag_send(k):
        for d in range(1, GT):
            tt = lax.rem(t + d, GT)
            go(remote(diag_cols(k, tt), diag_rows(k, t), d_send.at[k, d - 1], d_recv.at[k, d - 1], (tt, c)))

    def diag_wait(k):
        for d in range(1, GT):
            ref = diag_rows(k, lax.rem(t + GT - d, GT))
            pltpu.make_async_copy(ref, ref, d_recv.at[k, d - 1]).wait()

    def zi_src(k, h, tt):
        return zt.at[:, pl.ds(pl.multiple_of((2 * k + h) * TILE + tt * BAND, BAND), BAND)]

    def zi_dst(k, cc):
        return as_[k].at[pl.ds(pl.multiple_of(cc * MINE, MINE), MINE), pl.ds((k + 1) * 2 * RANK, BAND)]

    def zi_send(k):
        for h in range(2):
            @pl.loop(0, GT)
            def _(tt):
                here = jnp.logical_and(tt == t, t + GT * h == c)

                @pl.when(here)
                def _():
                    pltpu.make_async_copy(zi_src(k, h, tt), zi_dst(k, c), z_recv.at[k, c]).start()

                @pl.when(jnp.logical_not(here))
                def _():
                    remote(zi_src(k, h, tt), zi_dst(k, c), z_send.at[k, h * GT + tt], z_recv.at[k, c],
                           (tt, t + GT * h)).start()

    def zi_wait(k):
        @pl.loop(0, GC)
        def _(cc):
            ref = zi_dst(k, cc)
            pltpu.make_async_copy(ref, ref, z_recv.at[k, cc]).wait()

    def zi_sent(k):
        for h in range(2):
            @pl.loop(0, GT)
            def _(tt):
                @pl.when(jnp.logical_not(jnp.logical_and(tt == t, t + GT * h == c)))
                def _():
                    remote(zi_src(k, h, tt), zi_dst(k, c), z_send.at[k, h * GT + tt], z_recv.at[k, c],
                           (tt, t + GT * h)).wait_send()

    def right_copies(k):
        return [
            pltpu.make_async_copy(right.at[kk, 2 * k + jj], rs[k].at[jj, :, pl.ds((kk - k) * RANK, RANK)],
                                  loc_r.at[k, jj * NK + kk])
            for jj in range(2) for kk in range(k, NK)]

    def left_copies(k):
        return [
            pltpu.make_async_copy(left.at[k, j], bs[k].at[:, pl.ds(j * RANK, RANK)], loc_b.at[k, j])
            for j in range(2 * k + 2)]

    def z_copy(k):
        return pltpu.make_async_copy(zt.at[:, pl.ds(k * CHUNK, CHUNK)], block(k, c), loc_z.at[k])

    def d_copy(k):
        return pltpu.make_async_copy(diag_cols(k, t), diag_rows(k, t), loc_d.at[k])

    def coeffs(k):
        for cp in right_copies(k):
            cp.wait()
        z_copy(k).wait()
        n = NK - k
        lane = lax.broadcasted_iota(jnp.int32, (1, RANK), 1)
        for jj in range(2):
            @pl.loop(0, 2)
            def _(m):
                rows = pl.ds(pl.multiple_of(m * 256, 256), 256)
                acc = jnp.dot(zf[k, rows, pl.ds(jj * TILE, TILE)], rs[k][jj], preferred_element_type=F32)
                for i in range(n):
                    keep = lane < ranks[k + i, 2 * k + jj]
                    part = jnp.where(keep, acc[:, i * RANK:(i + 1) * RANK], 0.0)
                    as_[k + i][rows, pl.ds((2 * k + jj) * RANK, RANK)] = part.astype(BF16)

    def partial(k):
        for cp in left_copies(k):
            cp.wait()
        d_copy(k).wait()
        diag_wait(k)
        zi_wait(k)

        @pl.loop(0, TILE // 256)
        def _(n):
            cols = pl.ds(pl.multiple_of(n * 256, 256), 256)
            pt[k % 2, :, cols] = lax.dot_general(
                as_[k][...], bs[k][cols, :], (((1,), (1,)), ((), ())), preferred_element_type=F32)

    def rows_of(zz, half):
        return pl.ds(pl.multiple_of(lax.rem(zz + 4, 4) * 2 * OUTF + half * OUTF, OUTF), OUTF)

    def ship(k, i, value, dev):
        snd[k, i] = value.astype(BF16)
        go(remote(snd.at[k, i], rcv.at[k, i], s_send.at[k, i], s_recv.at[k, i], dev))

    def landed(k, i):
        ref = rcv.at[k, i]
        pltpu.make_async_copy(ref, ref, s_recv.at[k, i]).wait()
        return rcv[k, i].astype(F32)

    def sums_a(k):
        p = pt.at[k % 2]
        ship(k, 0, p[rows_of(z + 2, 0), :], zp)
        ship(k, 1, p[rows_of(z + 2, 1), :], zm)
        ship(k, 2, p[rows_of(z + 1, 1), :], zp)
        ship(k, 3, p[rows_of(z - 1, 0), :], zm)

    def sums_b(k):
        p = pt.at[k % 2]
        ship(k, 4, p[rows_of(z + 1, 0), :] + landed(k, 0), zp)
        ship(k, 5, p[rows_of(z - 1, 1), :] + landed(k, 1), zm)

    def sums_c(k):
        p = pt.at[k % 2]
        p[rows_of(z, 1), :] += landed(k, 2)
        p[rows_of(z, 0), :] += landed(k, 3)
        p[rows_of(z, 0), :] += landed(k, 4)
        p[rows_of(z, 1), :] += landed(k, 5)
        ship(k, 6, p[rows_of(z, 1 - yl), :], ylp)

    def sums_d(k):
        p = pt.at[k % 2]
        total = p[rows_of(z, yl), :] + landed(k, 6)
        out[:, pl.ds(k * TILE, TILE)] = total.astype(BF16)

    gather_a(0)
    for k in range(NK):
        z_copy(k).start()
        for cp in right_copies(k):
            cp.start()
    zi_send(0)
    diag_send(0)
    for k in range(NK):
        d_copy(k).start()
        for cp in left_copies(k):
            cp.start()
    gather_b(0)
    gather_a(1)
    for d in range(1, GC):
        g = lax.rem(c + d, GC)
        go(remote(wanted.at[g], asked.at[c], l_send.at[d - 1], l_recv.at[d - 1], (t, g)))
    own_list = pltpu.make_async_copy(wanted.at[c], asked.at[c], loc_l)
    own_list.start()
    zi_send(1)
    diag_send(1)
    gather_c(0)
    gather_d(0)
    coeffs(0)
    partial(0)
    sums_a(0)
    gather_b(1)
    gather_a(2)
    zi_send(2)
    diag_send(2)
    gather_c(1)
    sums_b(0)
    gather_d(1)
    coeffs(1)
    partial(1)
    sums_a(1)
    gather_b(2)
    sums_c(0)
    gather_c(2)
    sums_b(1)
    gather_d(2)
    coeffs(2)
    sums_d(0)
    partial(2)
    sums_a(2)
    sums_c(1)
    sums_b(2)
    sums_d(1)
    sums_c(2)
    sums_d(2)
    own_list.wait()
    for d in range(1, GC):
        ref = asked.at[lax.rem(c + GC - d, GC)]
        pltpu.make_async_copy(ref, ref, l_recv.at[d - 1]).wait()
    for cp in sent:
        cp.wait_send()
    for k in range(NK):
        zi_sent(k)


def sums_call(zt, left, right, ranks, diag, wanted):
    any_ = pl.BlockSpec(memory_space=pl.ANY)
    dma = pltpu.SemaphoreType.DMA
    return pl.pallas_call(
        sums_kernel,
        out_shape=(
            jax.ShapeDtypeStruct((OUTF, PTS), BF16),
            jax.ShapeDtypeStruct(wanted.shape, wanted.dtype),
        ),
        in_specs=[any_, any_, any_, pl.BlockSpec(memory_space=pltpu.SMEM), any_, any_],
        out_specs=(pl.BlockSpec(memory_space=pltpu.VMEM), any_),
        scratch_shapes=[
            pltpu.VMEM((NK, FIELDS, CHUNK), BF16),
            pltpu.VMEM((2, FIELDS, TILE), F32),
            *[pltpu.VMEM((TILE, 2 * RANK * (k + 1) + BAND), BF16) for k in range(NK)],
            *[pltpu.VMEM((FIELDS, 2 * RANK * (k + 1) + BAND), BF16) for k in range(NK)],
            *[pltpu.VMEM((2, TILE, RANK * (NK - k)), BF16) for k in range(NK)],
            pltpu.VMEM((NK, 7, OUTF, TILE), BF16),
            pltpu.VMEM((NK, 7, OUTF, TILE), BF16),
            dma((NK, 15)), dma((NK, 15)), dma((NK, GT - 1)), dma((NK, GT - 1)), dma((NK, GC)), dma((NK, GC)),
            dma((NK, 7)), dma((NK, 7)), dma((GC - 1,)), dma((GC - 1,)),
            dma((NK, 2 * NK)), dma((NK, 2 * NK)), dma((NK,)), dma((NK,)), dma,
        ],
        compiler_params=pltpu.CompilerParams(
            collective_id=0, has_side_effects=True, vmem_limit_bytes=60 * 1024 * 1024),
        cost_estimate=pl.CostEstimate(flops=17_000_000_000, bytes_accessed=20_000_000, transcendentals=0),
        name="tile_sums",
    )(zt, left, right, ranks, diag, wanted)


def grid_kernel(rows, asked, take, out, src, part, snd, rcv, res, send_sem, recv_sem, loc):
    t, c = place()
    barrier = pltpu.get_barrier_semaphore()
    for d in range(1, GC):
        pl.semaphore_signal(barrier, inc=1, device_id=(t, lax.rem(c + d, GC)), device_id_type=MESH)
    half = SLOT // 2
    src[...] = rows[...].astype(F32).T
    pl.semaphore_wait(barrier, GC - 1)

    def to(g, d):
        return pltpu.make_async_remote_copy(
            src_ref=snd.at[g], dst_ref=rcv.at[c], send_sem=send_sem.at[d], recv_sem=recv_sem.at[d],
            device_id=(t, g), device_id_type=MESH)

    def gather(idx_ref, base, n, from_, to_, to_base):
        @pl.loop(0, n // 16)
        def _(i):
            for u in range(16):
                r = i * 16 + u
                to_[pl.ds(to_base + r, 1), :] = from_[pl.ds(idx_ref[base + r], 1), :]

    @pl.loop(1, GC + 1)
    def _(d):
        g = lax.rem(c + d, GC)
        gather(asked, g * SLOT, SLOT, src, part, 0)
        packed = jnp.concatenate([part[pl.ds(0, half), :], part[pl.ds(half, half), :]], axis=1).astype(BF16)

        @pl.when(d < GC)
        def _():
            snd[g] = packed
            to(g, d - 1).start()

        @pl.when(d == GC)
        def _():
            rcv[c] = packed

    @pl.loop(0, GC)
    def _(d):
        s = lax.rem(c + GC - d, GC)

        @pl.when(d > 0)
        def _():
            ref = rcv.at[s]
            pltpu.make_async_copy(ref, ref, recv_sem.at[d - 1]).wait()

        got = rcv[s].astype(F32)
        src[pl.ds(pl.multiple_of(s * SLOT, SLOT), half), :] = got[:, :OUTF]
        src[pl.ds(pl.multiple_of(s * SLOT + half, half), half), :] = got[:, OUTF:]

    gather(take, 0, PTS, src, res, 0)
    out[...] = res[...].T.astype(BF16)

    @pl.loop(1, GC)
    def _(d):
        to(lax.rem(c + d, GC), d - 1).wait_send()


def grid_call(rows, asked, take):
    vmem = pl.BlockSpec(memory_space=pltpu.VMEM)
    smem = pl.BlockSpec(memory_space=pltpu.SMEM)
    dma = pltpu.SemaphoreType.DMA
    return pl.pallas_call(
        grid_kernel,
        out_shape=jax.ShapeDtypeStruct((OUTF, PTS), BF16),
        in_specs=[vmem, smem, smem],
        out_specs=vmem,
        scratch_shapes=[
            pltpu.VMEM((PTS, OUTF), F32),
            pltpu.VMEM((SLOT, OUTF), F32),
            pltpu.VMEM((GC, SLOT // 2, 2 * OUTF), BF16),
            pltpu.VMEM((GC, SLOT // 2, 2 * OUTF), BF16),
            pltpu.VMEM((PTS, OUTF), F32),
            dma((GC - 1,)), dma((GC - 1,)), dma,
        ],
        compiler_params=pltpu.CompilerParams(
            collective_id=1, has_side_effects=True, vmem_limit_bytes=40 * 1024 * 1024),
        name="grid_rows",
    )(rows, asked, take)


def row_lists(morton_of_grid):
    tile = morton_of_grid // TILE
    source = tile % GC
    row = tile // GC * TILE + morton_of_grid % TILE
    one = source[:, None] == jnp.arange(GC, dtype=jnp.int32)[None, :]
    cut = one.reshape(PTS // 128, 128, GC)
    below = jnp.tri(128, 128, -1, dtype=BF16)
    inside = jnp.einsum("ab,kbs->kas", below, cut.astype(BF16), preferred_element_type=F32)
    totals = jnp.sum(cut.astype(F32), axis=1)
    ahead = jnp.einsum("ab,bs->as", jnp.tri(PTS // 128, PTS // 128, -1, dtype=BF16), totals.astype(BF16),
                       preferred_element_type=F32)
    rank = jnp.sum(jnp.where(cut, inside + ahead[:, None, :], 0.0), axis=2).reshape(PTS).astype(jnp.int32)
    at = (rank[:, None] == jnp.arange(SLOT, dtype=jnp.int32)[None, :]).astype(BF16)
    high = jnp.where(one, (row // 128)[:, None], 0).astype(BF16)
    low = jnp.where(one, (row % 128)[:, None], 0).astype(BF16)
    both = jnp.einsum("ps,pr->sr", jnp.concatenate([high, low], axis=1), at, preferred_element_type=F32)
    both = both.astype(jnp.int32)
    wanted = both[:GC] * 128 + both[GC:]
    return wanted, source * SLOT + rank


def local(gaussian, left_basis, right_basis, tile_ranks, diag_factor, morton_of_grid):
    wanted, take = row_lists(morton_of_grid)
    wanted = jnp.pad(wanted.reshape(GC, SLOT // 128, 128), ((0, 0), (0, 8 - SLOT // 128), (0, 0)))
    rows, asked = sums_call(gaussian.T, left_basis, right_basis, tile_ranks, diag_factor, wanted)
    asked = asked[:, : SLOT // 128, :].reshape(PTS)
    return grid_call(rows, asked, take).T


def solution(mesh):
    placed = (
        P("trow", "tcol"),
        P("tcol", "trow", None, None),
        P("tcol", "trow", None, None),
        P("tcol", "trow"),
        P("tcol", "trow", None),
        P("tcol"),
    )
    return jax.shard_map(
        local, mesh=mesh, in_specs=placed, out_specs=P("tcol", "trow"), check_vma=False
    )
```

```python
import jax
import jax.numpy as jnp
from jax import lax
from jax.experimental import pallas as pl
from jax.experimental.pallas import tpu as pltpu
from jax.sharding import PartitionSpec as P

MESH = pl.DeviceIdType.MESH
F32 = jnp.float32
BF16 = jnp.bfloat16
TILE = 2048
RANK = 128
FIELDS = 512
NK = 3
GC = 16
GT = 8
MINE = FIELDS // GC
HALF = MINE // 2
ALL = FIELDS // 2
OUTF = FIELDS // GT
CHUNK = 2 * TILE
BAND = TILE // GT
PART = TILE // 4
PTS = NK * TILE
SLOT = PTS // GC


def place():
    t = lax.axis_index("trow")
    c = lax.axis_index("tcol")
    return t, c


def sums_kernel(
    zt, zb, left, right, ranks, diag, wanted,
    out, asked,
    zf, pt, b0, b1, b2, a0, a1, a2, r0, r1, r2, snd, rcv, zq, zi, dg,
    g_send, g_recv, d_send, d_recv, q_send, q_recv, i_send, i_recv, y_send, y_recv, s_send, s_recv, l_send, l_recv,
    loc_r, loc_b, loc_z, loc_d, loc_l, loc_q, loc_i,
):
    t, c = place()
    z, yl = t // 2, t % 2
    x, yh, core = c // 4, (c // 2) % 2, c % 2
    bs = (b0, b1, b2)
    as_ = (a0, a1, a2)
    rs = (r0, r1, r2)

    def cat(xx, yy, cc):
        return lax.rem(xx + 4, 4) * 4 + yy * 2 + cc

    def tat(zz, yy):
        return lax.rem(zz + 4, 4) * 2 + yy

    barrier = pltpu.get_barrier_semaphore()
    for d in range(1, GT):
        pl.semaphore_signal(barrier, inc=1, device_id=(lax.rem(t + d, GT), c), device_id_type=MESH)
    for d in range(1, GC):
        pl.semaphore_signal(barrier, inc=1, device_id=(t, lax.rem(c + d, GC)), device_id_type=MESH)
    pl.semaphore_wait(barrier, GT - 1 + GC - 1)

    def block(e, cc):
        rows = pl.ds(pl.multiple_of(cc * HALF, HALF), HALF)
        return zf.at[e, :, rows, :] if e < 2 else zf.at[2, e - 2, rows, :]

    def mine(e):
        cols = pl.ds(min(e, 2) * CHUNK, CHUNK)
        return zt.at[:, :, cols] if e < 2 else zt.at[e - 2, :, cols]

    def remote(src, dst, ssem, rsem, dev):
        return pltpu.make_async_remote_copy(
            src_ref=src, dst_ref=dst, send_sem=ssem, recv_sem=rsem, device_id=dev, device_id_type=MESH)

    sent = []

    def go(cp):
        cp.start()
        sent.append(cp)

    xp = (t, cat(x + 1, yh, core))
    xm = (t, cat(x - 1, yh, core))
    yp = (t, cat(x, 1 - yh, core))
    sib = (t, cat(x, yh, 1 - core))
    zp = (tat(z + 1, yl), c)
    zm = (tat(z - 1, yl), c)
    ylp = (tat(z, 1 - yl), c)

    def slot_block(i, cc):
        return (
            cat(x, 1 - yh, cc), cat(x - 1, yh, cc), cat(x + 1, yh, cc), cat(x - 1, 1 - yh, cc),
            cat(x + 1, 1 - yh, cc), cat(x - 2, yh, cc), cat(x + 2, 1 - yh, cc))[i]

    def fwd(k, i_block, src, i_send, slot, dev):
        go(remote(src, block(k, i_block), g_send.at[k, i_send], g_recv.at[k, slot], dev))

    def got(k, slot, cc):
        ref = block(k, cc)
        pltpu.make_async_copy(ref, ref, g_recv.at[k, slot]).wait()

    def gather_a(k):
        src = mine(k)
        fwd(k, c, src, 0, 0, yp)
        fwd(k, c, src, 2, 2, xm)

    def gather_e(k):
        src = mine(k)
        fwd(k, c, src, 1, 1, xp)
        fwd(k, c, src, 7, 7, sib)

    def relay(k, i, targets):
        cc = slot_block(i, core)
        got(k, i, cc)
        for i_send, slot, dev in targets:
            fwd(k, cc, block(k, cc), i_send, slot, dev)
        fwd(k, cc, block(k, cc), 8 + i, 8 + i, sib)

    def gather_b(k):
        relay(k, 0, ((3, 3, xp), (4, 4, xm)))
        relay(k, 1, ((5, 5, xp),))
        relay(k, 2, ())

    def gather_d(k):
        got(k, 7, cat(x, yh, 1 - core))
        for i in range(7):
            got(k, 8 + i, slot_block(i, 1 - core))

    def diag_cols(k, zz):
        return diag.at[k, :, pl.ds(pl.multiple_of(zz * PART, PART), PART)]

    def diag_rows(k, zz):
        return dg.at[k, pl.ds(pl.multiple_of(zz * BAND, BAND), BAND), :]

    def diag_send(k):
        for dz in (1, 3, 2):
            zz = lax.rem(z + dz, 4)
            go(remote(diag_cols(k, zz), diag_rows(k, z), d_send.at[k, dz - 1], d_recv.at[k, dz - 1], (tat(zz, yl), c)))

    def diag_wait(k):
        for dz in range(1, 4):
            ref = diag_rows(k, lax.rem(z + 4 - dz, 4))
            pltpu.make_async_copy(ref, ref, d_recv.at[k, dz - 1]).wait()

    def zi_first():
        pltpu.make_async_copy(zb.at[z], zq.at[z], loc_q).start()
        for dz in (1, 3, 2):
            zz = lax.rem(z + dz, 4)
            go(remote(zb.at[zz], zq.at[z], q_send.at[dz - 1], q_recv.at[dz - 1], (tat(zz, yl), c)))

    def zi_piece(g):
        return zq.at[(g % GT) // 2, :, :, pl.ds(pl.multiple_of(g // GT * NK * PART, NK * PART), NK * PART)]

    def zi_rows(cc):
        return zi.at[:, pl.ds(pl.multiple_of(cc * HALF, HALF), HALF), :]

    def zi_remote(d):
        g = lax.rem(2 * (c // 2) + 2 * d, GC) + yl
        return remote(zi_piece(g), zi_rows(c), i_send.at[d], i_recv.at[c], (t, g))

    def zi_second():
        pltpu.make_async_copy(zb.at[z], zq.at[z], loc_q).wait()
        for dz in range(1, 4):
            ref = zq.at[lax.rem(z + 4 - dz, 4)]
            pltpu.make_async_copy(ref, ref, q_recv.at[dz - 1]).wait()
        for d in range(1, GC // 2):
            go(zi_remote(d))

        @pl.when(core != yl)
        def _():
            zi_remote(0).start()

        @pl.when(core == yl)
        def _():
            pltpu.make_async_copy(zi_piece(c), zi_rows(c), i_recv.at[c]).start()

    def zi_cols(k):
        return zi.at[:, :, pl.ds(k * PART, PART)]

    def zi_pass(k):
        return remote(zi_cols(k), zi_cols(k), y_send.at[k], y_recv.at[k], ylp)

    def zi_third():
        @pl.when(core == yl)
        def _():
            @pl.loop(0, GC)
            def _(cc):
                pltpu.make_async_copy(zi_rows(cc), zi_rows(cc), i_recv.at[cc]).wait()

            zi_pass(0).start()

    def zi_more(k):
        @pl.when(core == yl)
        def _():
            zi_pass(k).start()

    def zi_wait(k):
        @pl.when(core != yl)
        def _():
            pltpu.make_async_copy(zi_cols(k), zi_cols(k), y_recv.at[k]).wait()

    def zi_sent():
        @pl.when(core != yl)
        def _():
            zi_remote(0).wait_send()

        @pl.when(core == yl)
        def _():
            for k in range(NK):
                zi_pass(k).wait_send()

    def right_copies(k):
        return [
            pltpu.make_async_copy(right.at[kk, 2 * k + jj], rs[k].at[jj, :, pl.ds((kk - k) * RANK, RANK)],
                                  loc_r.at[k, jj * NK + kk])
            for jj in range(2) for kk in range(k, NK)]

    def left_copies(k):
        return [
            pltpu.make_async_copy(left.at[k, j], bs[k].at[:, pl.ds(j * RANK, RANK)], loc_b.at[k, j])
            for j in range(2 * k + 2)]

    def z_copy(k):
        rows = pl.ds(pl.multiple_of(c * HALF, HALF), HALF)
        return pltpu.make_async_copy(zt.at[:, :, pl.ds(k * CHUNK, CHUNK)], zf.at[k, :, rows, :], loc_z.at[k])

    def d_copy(k):
        return pltpu.make_async_copy(diag_cols(k, z), diag_rows(k, z), loc_d.at[k])

    def coeffs(k, h=None):
        if h != 1:
            for cp in right_copies(k):
                cp.wait()
            z_copy(k).wait()
        n = NK - k
        lane = lax.broadcasted_iota(jnp.int32, (1, RANK), 1)
        for jj in range(2):
            def one(m):
                rows = pl.ds(m * ALL, ALL)
                acc = jnp.dot(zf[k, m, :, pl.ds(jj * TILE, TILE)], rs[k][jj], preferred_element_type=F32)
                for i in range(n):
                    keep = lane < ranks[k + i, 2 * k + jj]
                    part = jnp.where(keep, acc[:, i * RANK:(i + 1) * RANK], 0.0)
                    as_[k + i][rows, pl.ds((2 * k + jj) * RANK, RANK)] = part.astype(BF16)

            for m in range(2) if h is None else (h,):
                one(m)

    def partial(k, h=None):
        if h != 1:
            for cp in left_copies(k):
                cp.wait()
            d_copy(k).wait()
            diag_wait(k)
            zi_wait(k)
        halves = range(2) if h is None else (h,)

        @pl.loop(0, 4)
        def _(n):
            here = pl.ds(pl.multiple_of((2 * n + yl) * BAND, BAND), BAND)
            other = pl.ds(pl.multiple_of((2 * n + 1 - yl) * BAND, BAND), BAND)
            rows = pl.ds(pl.multiple_of(n * BAND, BAND), BAND)
            for m in halves:
                a = as_[k][pl.ds(m * ALL, ALL), :]
                pt[k % 2, m, :, other] = lax.dot_general(
                    a, bs[k][other, :], (((1,), (1,)), ((), ())), preferred_element_type=F32)
                pt[k % 2, m, :, here] = lax.dot_general(
                    a, bs[k][here, :], (((1,), (1,)), ((), ())), preferred_element_type=F32
                ) + lax.dot_general(
                    zi[m, :, pl.ds(k * PART, PART)], dg[k, rows, :], (((1,), (1,)), ((), ())),
                    preferred_element_type=F32)

    def held(e, zz, side):
        rows = pl.ds(pl.multiple_of((lax.rem(zz + 4, 4) * 2 + side) * MINE, MINE), MINE)
        return pt.at[e % 2, :, rows, :] if e < 2 else pt.at[0, e - 2, rows, :]

    def box(buf, e, i):
        return buf.at[e, i] if e < 2 else buf.at[2, i, e - 2]

    def ship(e, i, value, dev):
        ref = box(snd, e, i)
        ref[...] = value.astype(BF16)
        go(remote(ref, box(rcv, e, i), s_send.at[e, i], s_recv.at[e, i], dev))

    def landed(e, i):
        ref = box(rcv, e, i)
        pltpu.make_async_copy(ref, ref, s_recv.at[e, i]).wait()
        return ref[...].astype(F32)

    def sums_a(e):
        ship(e, 0, held(e, z + 2, 0)[...], zp)
        ship(e, 1, held(e, z + 2, 1)[...], zm)
        ship(e, 2, held(e, z + 1, 1)[...], zp)
        ship(e, 3, held(e, z - 1, 0)[...], zm)

    def sums_b(e):
        ship(e, 4, held(e, z + 1, 0)[...] + landed(e, 0), zp)
        ship(e, 5, held(e, z - 1, 1)[...] + landed(e, 1), zm)

    def sums_c(e):
        held(e, z, 1)[...] += landed(e, 2)
        held(e, z, 0)[...] += landed(e, 3)
        held(e, z, 0)[...] += landed(e, 4)
        held(e, z, 1)[...] += landed(e, 5)
        ship(e, 6, held(e, z, 1 - yl)[...], ylp)

    def sums_d(e):
        total = (held(e, z, yl)[...] + landed(e, 6)).astype(BF16)
        cols = pl.ds(min(e, 2) * TILE, TILE)
        for q in range(2):
            if e < 2:
                for h in range(2):
                    out[pl.ds(q * MINE + h * HALF, HALF), cols] = total[h, q * HALF:(q + 1) * HALF]
            else:
                out[pl.ds(q * MINE + (e - 2) * HALF, HALF), cols] = total[q * HALF:(q + 1) * HALF]

    def list_send():
        for d in range(1, GC):
            g = lax.rem(c + d, GC)
            go(remote(wanted.at[g], asked.at[c], l_send.at[d - 1], l_recv.at[d - 1], (t, g)))

    gather_a(0)
    gather_e(0)
    zi_first()
    diag_send(0)
    z_copy(0).start()
    for cp in right_copies(0):
        cp.start()
    gather_b(0)
    zi_second()
    gather_a(1)
    relay(0, 3, ())
    gather_e(1)
    relay(0, 4, ((6, 6, xm),))
    diag_send(1)
    for k in range(NK):
        d_copy(k).start()
        for cp in left_copies(k):
            cp.start()
        if k:
            z_copy(k).start()
            for cp in right_copies(k):
                cp.start()
    own_list = pltpu.make_async_copy(wanted.at[c], asked.at[c], loc_l)
    own_list.start()
    list_send()
    zi_third()
    relay(0, 5, ())
    relay(0, 6, ())
    gather_d(0)
    coeffs(0)
    gather_b(1)
    gather_a(2)
    diag_send(2)
    partial(0)
    sums_a(0)
    relay(1, 3, ())
    gather_e(2)
    relay(1, 4, ((6, 6, xm),))
    zi_more(1)
    sums_b(0)
    relay(1, 5, ())
    relay(1, 6, ())
    gather_d(1)
    coeffs(1)
    gather_b(2)
    gather_a(3)
    zi_more(2)
    partial(1)
    sums_a(1)
    relay(2, 3, ())
    gather_e(3)
    relay(2, 4, ((6, 6, xm),))
    sums_c(0)
    relay(2, 5, ())
    relay(2, 6, ())
    gather_d(2)
    coeffs(2, 0)
    gather_b(3)
    sums_b(1)
    sums_d(0)
    partial(2, 0)
    sums_a(2)
    relay(3, 3, ())
    relay(3, 4, ((6, 6, xm),))
    relay(3, 5, ())
    relay(3, 6, ())
    sums_c(1)
    gather_d(3)
    coeffs(2, 1)
    sums_b(2)
    partial(2, 1)
    sums_a(3)
    sums_d(1)
    sums_c(2)
    sums_b(3)
    sums_d(2)
    sums_c(3)
    sums_d(3)
    own_list.wait()
    for d in range(1, GC):
        ref = asked.at[lax.rem(c + GC - d, GC)]
        pltpu.make_async_copy(ref, ref, l_recv.at[d - 1]).wait()
    for cp in sent:
        cp.wait_send()
    zi_sent()


def sums_call(zt, zb, left, right, ranks, diag, wanted):
    any_ = pl.BlockSpec(memory_space=pl.ANY)
    dma = pltpu.SemaphoreType.DMA
    return pl.pallas_call(
        sums_kernel,
        out_shape=(
            jax.ShapeDtypeStruct((OUTF, PTS), BF16),
            jax.ShapeDtypeStruct(wanted.shape, wanted.dtype),
        ),
        in_specs=[any_, any_, any_, any_, pl.BlockSpec(memory_space=pltpu.SMEM), any_, any_],
        out_specs=(pl.BlockSpec(memory_space=pltpu.VMEM), any_),
        scratch_shapes=[
            pltpu.VMEM((NK, 2, ALL, CHUNK), BF16),
            pltpu.VMEM((2, 2, ALL, TILE), F32),
            *[pltpu.VMEM((TILE, 2 * RANK * (k + 1)), BF16) for k in range(NK)],
            *[pltpu.VMEM((FIELDS, 2 * RANK * (k + 1)), BF16) for k in range(NK)],
            *[pltpu.VMEM((2, TILE, RANK * (NK - k)), BF16) for k in range(NK)],
            pltpu.VMEM((NK, 7, 2, MINE, TILE), BF16),
            pltpu.VMEM((NK, 7, 2, MINE, TILE), BF16),
            pltpu.VMEM((4, 2, HALF, 2 * NK * PART), BF16),
            pltpu.VMEM((2, ALL, NK * PART), BF16),
            pltpu.VMEM((NK, 4 * BAND, PART), BF16),
            dma((4, 15)), dma((4, 15)), dma((NK, 3)), dma((NK, 3)),
            dma((3,)), dma((3,)), dma((GC // 2,)), dma((GC,)), dma((NK,)), dma((NK,)),
            dma((4, 7)), dma((4, 7)), dma((GC - 1,)), dma((GC - 1,)),
            dma((NK, 2 * NK)), dma((NK, 2 * NK)), dma((NK,)), dma((NK,)), dma, dma, dma,
        ],
        compiler_params=pltpu.CompilerParams(
            collective_id=0, has_side_effects=True, vmem_limit_bytes=60 * 1024 * 1024),
        cost_estimate=pl.CostEstimate(flops=17_000_000_000, bytes_accessed=20_000_000, transcendentals=0),
        name="tile_sums",
    )(zt, zb, left, right, ranks, diag, wanted)


def grid_kernel(rows, asked, take, out, src, part, snd, rcv, res, send_sem, recv_sem, loc):
    t, c = place()
    barrier = pltpu.get_barrier_semaphore()
    for d in range(1, GC):
        pl.semaphore_signal(barrier, inc=1, device_id=(t, lax.rem(c + d, GC)), device_id_type=MESH)
    half = SLOT // 2
    src[...] = rows[...].astype(F32).T
    pl.semaphore_wait(barrier, GC - 1)

    def to(g, d):
        return pltpu.make_async_remote_copy(
            src_ref=snd.at[g], dst_ref=rcv.at[c], send_sem=send_sem.at[d], recv_sem=recv_sem.at[d],
            device_id=(t, g), device_id_type=MESH)

    def gather(idx_ref, base, n, from_, to_):
        @pl.loop(0, n // 16)
        def _(i):
            for u in range(16):
                r = i * 16 + u
                to_[pl.ds(r, 1), :] = from_[pl.ds(idx_ref[base + r], 1), :]

    @pl.loop(1, GC + 1)
    def _(d):
        g = lax.rem(c + d, GC)
        gather(asked, g * 1024, SLOT, src, part)
        packed = jnp.concatenate([part[pl.ds(0, half), :], part[pl.ds(half, half), :]], axis=1).astype(BF16)

        @pl.when(d < GC)
        def _():
            snd[g] = packed
            to(g, d - 1).start()

        @pl.when(d == GC)
        def _():
            rcv[c] = packed

    @pl.loop(0, GC)
    def _(d):
        s = lax.rem(c + GC - d, GC)

        @pl.when(d > 0)
        def _():
            ref = rcv.at[s]
            pltpu.make_async_copy(ref, ref, recv_sem.at[d - 1]).wait()

        got = rcv[s].astype(F32)
        src[pl.ds(pl.multiple_of(s * SLOT, SLOT), half), :] = got[:, :OUTF]
        src[pl.ds(pl.multiple_of(s * SLOT + half, half), half), :] = got[:, OUTF:]

    gather(take, 0, PTS, src, res)
    out[...] = res[...].T.astype(BF16)

    @pl.loop(1, GC)
    def _(d):
        to(lax.rem(c + d, GC), d - 1).wait_send()


def grid_call(rows, asked, take):
    vmem = pl.BlockSpec(memory_space=pltpu.VMEM)
    smem = pl.BlockSpec(memory_space=pltpu.SMEM)
    dma = pltpu.SemaphoreType.DMA
    return pl.pallas_call(
        grid_kernel,
        out_shape=jax.ShapeDtypeStruct((OUTF, PTS), BF16),
        in_specs=[vmem, smem, smem],
        out_specs=vmem,
        scratch_shapes=[
            pltpu.VMEM((PTS, OUTF), F32),
            pltpu.VMEM((SLOT, OUTF), F32),
            pltpu.VMEM((GC, SLOT // 2, 2 * OUTF), BF16),
            pltpu.VMEM((GC, SLOT // 2, 2 * OUTF), BF16),
            pltpu.VMEM((PTS, OUTF), F32),
            dma((GC - 1,)), dma((GC - 1,)), dma,
        ],
        compiler_params=pltpu.CompilerParams(
            collective_id=1, has_side_effects=True, vmem_limit_bytes=40 * 1024 * 1024),
        name="grid_rows",
    )(rows, asked, take)


def row_lists(morton_of_grid):
    tile = morton_of_grid // TILE
    source = tile % GC
    row = tile // GC * TILE + morton_of_grid % TILE
    one = source[:, None] == jnp.arange(GC, dtype=jnp.int32)[None, :]
    cut = one.reshape(PTS // 128, 128, GC)
    below = jnp.tri(128, 128, -1, dtype=BF16)
    inside = jnp.einsum("ab,kbs->kas", below, cut.astype(BF16), preferred_element_type=F32)
    totals = jnp.sum(cut.astype(F32), axis=1)
    ahead = jnp.einsum("ab,bs->as", jnp.tri(PTS // 128, PTS // 128, -1, dtype=BF16), totals.astype(BF16),
                       preferred_element_type=F32)
    rank = jnp.sum(jnp.where(cut, inside + ahead[:, None, :], 0.0), axis=2).reshape(PTS).astype(jnp.int32)
    at = (rank[:, None] == jnp.arange(SLOT, dtype=jnp.int32)[None, :]).astype(BF16)
    high = jnp.where(one, (row // 128)[:, None], 0).astype(BF16)
    low = jnp.where(one, (row % 128)[:, None], 0).astype(BF16)
    both = jnp.einsum("ps,pr->sr", jnp.concatenate([high, low], axis=1), at, preferred_element_type=F32)
    both = both.astype(jnp.int32)
    wanted = both[:GC] * 128 + both[GC:]
    return wanted, source * SLOT + rank


def local(gaussian, left_basis, right_basis, tile_ranks, diag_factor, morton_of_grid):
    wanted, take = row_lists(morton_of_grid)
    wanted = jnp.pad(wanted.reshape(GC, SLOT // 128, 128), ((0, 0), (0, 8 - SLOT // 128), (0, 0)))
    zt = gaussian.T
    zb = zt.reshape(MINE, NK, 2, 4, PART).transpose(3, 0, 2, 1, 4).reshape(4, 2, HALF, 2 * NK * PART)
    zt = zt.reshape(2, HALF, NK * CHUNK)
    rows, asked = sums_call(zt, zb, left_basis, right_basis, tile_ranks, diag_factor, wanted)
    return grid_call(rows, asked.reshape(GC * 1024), take).T


def solution(mesh):
    placed = (
        P("trow", "tcol"),
        P("tcol", "trow", None, None),
        P("tcol", "trow", None, None),
        P("tcol", "trow"),
        P("tcol", "trow", None),
        P("tcol"),
    )
    return jax.shard_map(
        local, mesh=mesh, in_specs=placed, out_specs=P("tcol", "trow"), check_vma=False
    )
```

```python
import jax
import jax.numpy as jnp
from jax import lax
from jax.experimental import pallas as pl
from jax.experimental.pallas import tpu as pltpu
from jax.sharding import PartitionSpec as P

MESH = pl.DeviceIdType.MESH
F32 = jnp.float32
BF16 = jnp.bfloat16
TILE = 2048
RANK = 128
FIELDS = 512
NK = 3
GC = 16
GT = 8
MINE = FIELDS // GC
HALF = MINE // 2
ALL = FIELDS // 2
OUTF = FIELDS // GT
CHUNK = 2 * TILE
BAND = TILE // GT
PART = TILE // 4
PTS = NK * TILE
SLOT = PTS // GC


def place():
    t = lax.axis_index("trow")
    c = lax.axis_index("tcol")
    return t, c


def sums_kernel(
    zt, left, right, ranks, diag, morton,
    out, asked, take,
    zf, pt, b0, b1, b2, a0, a1, a2, r0, r1, r2, snd, rcv, zq, zi, dg, wanted,
    g_send, g_recv, d_send, d_recv, q_send, q_recv, i_send, i_recv, y_send, y_recv, s_send, s_recv, l_send, l_recv,
    loc_r, loc_b, loc_z, loc_d, loc_l, loc_q,
):
    t, c = place()
    z, yl = t // 2, t % 2
    x, yh, core = c // 4, (c // 2) % 2, c % 2
    bs = (b0, b1, b2)
    as_ = (a0, a1, a2)
    rs = (r0, r1, r2)

    def cat(xx, yy, cc):
        return lax.rem(xx + 4, 4) * 4 + yy * 2 + cc

    def tat(zz, yy):
        return lax.rem(zz + 4, 4) * 2 + yy

    barrier = pltpu.get_barrier_semaphore()
    for d in range(1, GT):
        pl.semaphore_signal(barrier, inc=1, device_id=(lax.rem(t + d, GT), c), device_id_type=MESH)
    for d in range(1, GC):
        pl.semaphore_signal(barrier, inc=1, device_id=(t, lax.rem(c + d, GC)), device_id_type=MESH)
    pl.semaphore_wait(barrier, GT - 1 + GC - 1)

    def block(e, cc):
        rows = pl.ds(pl.multiple_of(cc * HALF, HALF), HALF)
        return zf.at[e, :, rows, :] if e < 2 else zf.at[2, e - 2, rows, :]

    def mine(e):
        cols = pl.ds(min(e, 2) * CHUNK, CHUNK)
        return zt.at[:, :, cols] if e < 2 else zt.at[e - 2, :, cols]

    def remote(src, dst, ssem, rsem, dev):
        return pltpu.make_async_remote_copy(
            src_ref=src, dst_ref=dst, send_sem=ssem, recv_sem=rsem, device_id=dev, device_id_type=MESH)

    sent = []

    def go(cp):
        cp.start()
        sent.append(cp)

    xp = (t, cat(x + 1, yh, core))
    xm = (t, cat(x - 1, yh, core))
    yp = (t, cat(x, 1 - yh, core))
    sib = (t, cat(x, yh, 1 - core))
    zp = (tat(z + 1, yl), c)
    zm = (tat(z - 1, yl), c)
    ylp = (tat(z, 1 - yl), c)

    def slot_block(i, cc):
        return (
            cat(x, 1 - yh, cc), cat(x - 1, yh, cc), cat(x + 1, yh, cc), cat(x - 1, 1 - yh, cc),
            cat(x + 1, 1 - yh, cc), cat(x - 2, yh, cc), cat(x + 2, 1 - yh, cc))[i]

    def fwd(k, i_block, src, i_send, slot, dev):
        go(remote(src, block(k, i_block), g_send.at[k, i_send], g_recv.at[k, slot], dev))

    def got(k, slot, cc):
        ref = block(k, cc)
        pltpu.make_async_copy(ref, ref, g_recv.at[k, slot]).wait()

    def gather_a(k):
        src = mine(k)
        fwd(k, c, src, 0, 0, yp)
        fwd(k, c, src, 2, 2, xm)

    def gather_e(k):
        src = mine(k)
        fwd(k, c, src, 1, 1, xp)
        fwd(k, c, src, 7, 7, sib)

    def relay(k, i, targets):
        cc = slot_block(i, core)
        got(k, i, cc)
        for i_send, slot, dev in targets:
            fwd(k, cc, block(k, cc), i_send, slot, dev)
        fwd(k, cc, block(k, cc), 8 + i, 8 + i, sib)

    def gather_b(k):
        relay(k, 0, ((3, 3, xp), (4, 4, xm)))
        relay(k, 1, ((5, 5, xp),))
        relay(k, 2, ())

    def gather_d(k):
        got(k, 7, cat(x, yh, 1 - core))
        for i in range(7):
            got(k, 8 + i, slot_block(i, 1 - core))

    def diag_cols(k, zz):
        return diag.at[k, :, pl.ds(pl.multiple_of(zz * PART, PART), PART)]

    def diag_rows(k, zz):
        return dg.at[k, pl.ds(pl.multiple_of(zz * BAND, BAND), BAND), :]

    def diag_send(k):
        for dz in (1, 3, 2):
            zz = lax.rem(z + dz, 4)
            go(remote(diag_cols(k, zz), diag_rows(k, z), d_send.at[k, dz - 1], d_recv.at[k, dz - 1], (tat(zz, yl), c)))

    def diag_wait(k):
        for dz in range(1, 4):
            ref = diag_rows(k, lax.rem(z + 4 - dz, 4))
            pltpu.make_async_copy(ref, ref, d_recv.at[k, dz - 1]).wait()

    def zi_from(k, h, zz):
        return zt.at[:, :, pl.ds(pl.multiple_of((2 * k + h) * TILE + zz * PART, PART), PART)]

    def zi_at(k, h, zz):
        return zq.at[zz, :, :, pl.ds((h * NK + k) * PART, PART)]

    def zi_first():
        for k in range(NK):
            for h in range(2):
                i = h * NK + k
                pltpu.make_async_copy(zi_from(k, h, z), zi_at(k, h, z), loc_q.at[i]).start()
                for dz in (1, 3, 2):
                    zz = lax.rem(z + dz, 4)
                    go(remote(zi_from(k, h, zz), zi_at(k, h, z), q_send.at[dz - 1, i], q_recv.at[dz - 1, i],
                              (tat(zz, yl), c)))

    def zi_piece(g):
        return zq.at[(g % GT) // 2, :, :, pl.ds(pl.multiple_of(g // GT * NK * PART, NK * PART), NK * PART)]

    def zi_rows(cc):
        return zi.at[:, pl.ds(pl.multiple_of(cc * HALF, HALF), HALF), :]

    def zi_remote(d):
        g = lax.rem(2 * (c // 2) + 2 * d, GC) + yl
        return remote(zi_piece(g), zi_rows(c), i_send.at[d], i_recv.at[c], (t, g))

    def zi_second():
        for k in range(NK):
            for h in range(2):
                i = h * NK + k
                pltpu.make_async_copy(zi_from(k, h, z), zi_at(k, h, z), loc_q.at[i]).wait()
                for dz in range(1, 4):
                    ref = zi_at(k, h, lax.rem(z + 4 - dz, 4))
                    pltpu.make_async_copy(ref, ref, q_recv.at[dz - 1, i]).wait()
        for d in range(1, GC // 2):
            go(zi_remote(d))

        @pl.when(core != yl)
        def _():
            zi_remote(0).start()

        @pl.when(core == yl)
        def _():
            pltpu.make_async_copy(zi_piece(c), zi_rows(c), i_recv.at[c]).start()

    def zi_cols(k):
        return zi.at[:, :, pl.ds(k * PART, PART)]

    def zi_pass(k):
        return remote(zi_cols(k), zi_cols(k), y_send.at[k], y_recv.at[k], ylp)

    def zi_third():
        @pl.when(core == yl)
        def _():
            @pl.loop(0, GC)
            def _(cc):
                pltpu.make_async_copy(zi_rows(cc), zi_rows(cc), i_recv.at[cc]).wait()

            zi_pass(0).start()

    def zi_more(k):
        @pl.when(core == yl)
        def _():
            zi_pass(k).start()

    def zi_wait(k):
        @pl.when(core != yl)
        def _():
            pltpu.make_async_copy(zi_cols(k), zi_cols(k), y_recv.at[k]).wait()

    def zi_sent():
        @pl.when(core != yl)
        def _():
            zi_remote(0).wait_send()

        @pl.when(core == yl)
        def _():
            for k in range(NK):
                zi_pass(k).wait_send()

    def right_copies(k):
        return [
            pltpu.make_async_copy(right.at[kk, 2 * k + jj], rs[k].at[jj, :, pl.ds((kk - k) * RANK, RANK)],
                                  loc_r.at[k, jj * NK + kk])
            for jj in range(2) for kk in range(k, NK)]

    def left_copies(k):
        return [
            pltpu.make_async_copy(left.at[k, j], bs[k].at[:, pl.ds(j * RANK, RANK)], loc_b.at[k, j])
            for j in range(2 * k + 2)]

    def z_copy(k):
        rows = pl.ds(pl.multiple_of(c * HALF, HALF), HALF)
        return pltpu.make_async_copy(zt.at[:, :, pl.ds(k * CHUNK, CHUNK)], zf.at[k, :, rows, :], loc_z.at[k])

    def d_copy(k):
        return pltpu.make_async_copy(diag_cols(k, z), diag_rows(k, z), loc_d.at[k])

    def coeffs(k, h=None):
        if h != 1:
            for cp in right_copies(k):
                cp.wait()
            z_copy(k).wait()
        n = NK - k
        lane = lax.broadcasted_iota(jnp.int32, (1, RANK), 1)
        for jj in range(2):
            def one(m):
                rows = pl.ds(m * ALL, ALL)
                acc = jnp.dot(zf[k, m, :, pl.ds(jj * TILE, TILE)], rs[k][jj], preferred_element_type=F32)
                for i in range(n):
                    keep = lane < ranks[k + i, 2 * k + jj]
                    part = jnp.where(keep, acc[:, i * RANK:(i + 1) * RANK], 0.0)
                    as_[k + i][rows, pl.ds((2 * k + jj) * RANK, RANK)] = part.astype(BF16)

            for m in range(2) if h is None else (h,):
                one(m)

    def partial(k, h=None):
        if h != 1:
            for cp in left_copies(k):
                cp.wait()
            d_copy(k).wait()
            diag_wait(k)
            zi_wait(k)
        halves = range(2) if h is None else (h,)

        @pl.loop(0, 4)
        def _(n):
            here = pl.ds(pl.multiple_of((2 * n + yl) * BAND, BAND), BAND)
            other = pl.ds(pl.multiple_of((2 * n + 1 - yl) * BAND, BAND), BAND)
            rows = pl.ds(pl.multiple_of(n * BAND, BAND), BAND)
            for m in halves:
                a = as_[k][pl.ds(m * ALL, ALL), :]
                pt[k % 2, m, :, other] = lax.dot_general(
                    a, bs[k][other, :], (((1,), (1,)), ((), ())), preferred_element_type=F32)
                pt[k % 2, m, :, here] = lax.dot_general(
                    a, bs[k][here, :], (((1,), (1,)), ((), ())), preferred_element_type=F32
                ) + lax.dot_general(
                    zi[m, :, pl.ds(k * PART, PART)], dg[k, rows, :], (((1,), (1,)), ((), ())),
                    preferred_element_type=F32)

    def held(e, zz, side):
        rows = pl.ds(pl.multiple_of((lax.rem(zz + 4, 4) * 2 + side) * MINE, MINE), MINE)
        return pt.at[e % 2, :, rows, :] if e < 2 else pt.at[0, e - 2, rows, :]

    def box(buf, e, i):
        return buf.at[e, i] if e < 2 else buf.at[2, i, e - 2]

    def ship(e, i, value, dev):
        ref = box(snd, e, i)
        ref[...] = value.astype(BF16)
        go(remote(ref, box(rcv, e, i), s_send.at[e, i], s_recv.at[e, i], dev))

    def landed(e, i):
        ref = box(rcv, e, i)
        pltpu.make_async_copy(ref, ref, s_recv.at[e, i]).wait()
        return ref[...].astype(F32)

    def sums_a(e):
        ship(e, 0, held(e, z + 2, 0)[...], zp)
        ship(e, 1, held(e, z + 2, 1)[...], zm)
        ship(e, 2, held(e, z + 1, 1)[...], zp)
        ship(e, 3, held(e, z - 1, 0)[...], zm)

    def sums_b(e):
        ship(e, 4, held(e, z + 1, 0)[...] + landed(e, 0), zp)
        ship(e, 5, held(e, z - 1, 1)[...] + landed(e, 1), zm)

    def sums_c(e):
        held(e, z, 1)[...] += landed(e, 2)
        held(e, z, 0)[...] += landed(e, 3)
        held(e, z, 0)[...] += landed(e, 4)
        held(e, z, 1)[...] += landed(e, 5)
        ship(e, 6, held(e, z, 1 - yl)[...], ylp)

    def sums_d(e):
        total = (held(e, z, yl)[...] + landed(e, 6)).astype(BF16)
        cols = pl.ds(min(e, 2) * TILE, TILE)
        for q in range(2):
            if e < 2:
                for h in range(2):
                    out[pl.ds(q * MINE + h * HALF, HALF), cols] = total[h, q * HALF:(q + 1) * HALF]
            else:
                out[pl.ds(q * MINE + (e - 2) * HALF, HALF), cols] = total[q * HALF:(q + 1) * HALF]

    def lists():
        m = morton[...]
        tile = m // TILE
        source = tile % GC
        row = tile // GC * TILE + m % TILE
        lane = lax.broadcasted_iota(jnp.int32, (128, 128), 1)
        before = (lax.broadcasted_iota(jnp.int32, (128, 128), 0) < lane).astype(BF16)
        n = PTS // 128
        above = (lax.broadcasted_iota(jnp.int32, (n, n), 1) < lax.broadcasted_iota(jnp.int32, (n, n), 0)).astype(BF16)
        rank = jnp.zeros((n, 128), F32)
        for g in range(GC):
            one = (source == g).astype(F32)
            ones = one.astype(BF16)
            inside = jnp.dot(ones, before, preferred_element_type=F32)
            ahead = jnp.sum(jnp.dot(above, ones, preferred_element_type=F32), axis=1, keepdims=True)
            rank = rank + one * (inside + ahead)
        rank = rank.astype(jnp.int32)
        take[...] = source * SLOT + rank
        group = lax.broadcasted_iota(jnp.int32, (GC, 128), 0)
        spot = lax.broadcasted_iota(jnp.int32, (SLOT, 128), 0)
        both = jnp.zeros((2 * GC, SLOT), F32)
        for i in range(n):
            at = (spot == rank[i:i + 1]).astype(F32).astype(BF16)
            here = group == source[i:i + 1]
            high = jnp.where(here, row[i:i + 1] // 128, 0)
            low = jnp.where(here, row[i:i + 1] % 128, 0)
            pair = jnp.concatenate([high, low], axis=0).astype(F32).astype(BF16)
            both = both + lax.dot_general(pair, at, (((1,), (1,)), ((), ())), preferred_element_type=F32)
        both = both.astype(jnp.int32)
        rows = both[:GC] * 128 + both[GC:]
        wanted[...] = jnp.zeros_like(wanted)
        for q in range(SLOT // 128):
            wanted[:, q, :] = rows[:, q * 128:(q + 1) * 128]

    def list_send():
        for d in range(1, GC):
            g = lax.rem(c + d, GC)
            go(remote(wanted.at[g], asked.at[c], l_send.at[d - 1], l_recv.at[d - 1], (t, g)))

    gather_a(0)
    gather_e(0)
    zi_first()
    diag_send(0)
    z_copy(0).start()
    for cp in right_copies(0):
        cp.start()
    gather_b(0)
    zi_second()
    gather_a(1)
    relay(0, 3, ())
    gather_e(1)
    relay(0, 4, ((6, 6, xm),))
    diag_send(1)
    for k in range(NK):
        d_copy(k).start()
        for cp in left_copies(k):
            cp.start()
        if k:
            z_copy(k).start()
            for cp in right_copies(k):
                cp.start()
    zi_third()
    relay(0, 5, ())
    relay(0, 6, ())
    lists()
    own_list = pltpu.make_async_copy(wanted.at[c], asked.at[c], loc_l)
    own_list.start()
    list_send()
    gather_d(0)
    coeffs(0)
    gather_b(1)
    gather_a(2)
    diag_send(2)
    partial(0)
    sums_a(0)
    relay(1, 3, ())
    gather_e(2)
    relay(1, 4, ((6, 6, xm),))
    zi_more(1)
    sums_b(0)
    relay(1, 5, ())
    relay(1, 6, ())
    gather_d(1)
    coeffs(1)
    gather_b(2)
    gather_a(3)
    zi_more(2)
    partial(1)
    sums_a(1)
    relay(2, 3, ())
    gather_e(3)
    relay(2, 4, ((6, 6, xm),))
    sums_c(0)
    relay(2, 5, ())
    relay(2, 6, ())
    gather_d(2)
    coeffs(2, 0)
    gather_b(3)
    sums_b(1)
    sums_d(0)
    partial(2, 0)
    sums_a(2)
    relay(3, 3, ())
    relay(3, 4, ((6, 6, xm),))
    relay(3, 5, ())
    relay(3, 6, ())
    sums_c(1)
    gather_d(3)
    coeffs(2, 1)
    sums_b(2)
    partial(2, 1)
    sums_a(3)
    sums_d(1)
    sums_c(2)
    sums_b(3)
    sums_d(2)
    sums_c(3)
    sums_d(3)
    own_list.wait()
    for d in range(1, GC):
        ref = asked.at[lax.rem(c + GC - d, GC)]
        pltpu.make_async_copy(ref, ref, l_recv.at[d - 1]).wait()
    for cp in sent:
        cp.wait_send()
    zi_sent()


def sums_call(zt, left, right, ranks, diag, morton):
    any_ = pl.BlockSpec(memory_space=pl.ANY)
    vmem = pl.BlockSpec(memory_space=pltpu.VMEM)
    dma = pltpu.SemaphoreType.DMA
    return pl.pallas_call(
        sums_kernel,
        out_shape=(
            jax.ShapeDtypeStruct((OUTF, PTS), BF16),
            jax.ShapeDtypeStruct((GC, 8, 128), jnp.int32),
            jax.ShapeDtypeStruct((PTS // 128, 128), jnp.int32),
        ),
        in_specs=[any_, any_, any_, pl.BlockSpec(memory_space=pltpu.SMEM), any_, vmem],
        out_specs=(vmem, any_, vmem),
        scratch_shapes=[
            pltpu.VMEM((NK, 2, ALL, CHUNK), BF16),
            pltpu.VMEM((2, 2, ALL, TILE), F32),
            *[pltpu.VMEM((TILE, 2 * RANK * (k + 1)), BF16) for k in range(NK)],
            *[pltpu.VMEM((FIELDS, 2 * RANK * (k + 1)), BF16) for k in range(NK)],
            *[pltpu.VMEM((2, TILE, RANK * (NK - k)), BF16) for k in range(NK)],
            pltpu.VMEM((NK, 7, 2, MINE, TILE), BF16),
            pltpu.VMEM((NK, 7, 2, MINE, TILE), BF16),
            pltpu.VMEM((4, 2, HALF, 2 * NK * PART), BF16),
            pltpu.VMEM((2, ALL, NK * PART), BF16),
            pltpu.VMEM((NK, 4 * BAND, PART), BF16),
            pltpu.VMEM((GC, 8, 128), jnp.int32),
            dma((4, 15)), dma((4, 15)), dma((NK, 3)), dma((NK, 3)),
            dma((3, 2 * NK)), dma((3, 2 * NK)), dma((GC // 2,)), dma((GC,)), dma((NK,)), dma((NK,)),
            dma((4, 7)), dma((4, 7)), dma((GC - 1,)), dma((GC - 1,)),
            dma((NK, 2 * NK)), dma((NK, 2 * NK)), dma((NK,)), dma((NK,)), dma, dma((2 * NK,)),
        ],
        compiler_params=pltpu.CompilerParams(
            collective_id=0, has_side_effects=True, vmem_limit_bytes=60 * 1024 * 1024),
        cost_estimate=pl.CostEstimate(flops=17_000_000_000, bytes_accessed=20_000_000, transcendentals=0),
        name="tile_sums",
    )(zt, left, right, ranks, diag, morton)


def grid_kernel(rows, asked_in, take_in, out, asked, take, src, part, snd, rcv, res, send_sem, recv_sem, loc):
    t, c = place()
    barrier = pltpu.get_barrier_semaphore()
    for d in range(1, GC):
        pl.semaphore_signal(barrier, inc=1, device_id=(t, lax.rem(c + d, GC)), device_id_type=MESH)
    half = SLOT // 2
    fetch_asked = pltpu.make_async_copy(asked_in, asked, loc.at[0])
    fetch_asked.start()
    fetch_take = pltpu.make_async_copy(take_in, take, loc.at[1])
    fetch_take.start()
    src[...] = rows[...].astype(F32).T
    fetch_asked.wait()
    fetch_take.wait()
    pl.semaphore_wait(barrier, GC - 1)

    def to(g, d):
        return pltpu.make_async_remote_copy(
            src_ref=snd.at[g], dst_ref=rcv.at[c], send_sem=send_sem.at[d], recv_sem=recv_sem.at[d],
            device_id=(t, g), device_id_type=MESH)

    def gather(idx_ref, base, n, from_, to_):
        @pl.loop(0, n // 16)
        def _(i):
            for u in range(16):
                r = i * 16 + u
                to_[pl.ds(r, 1), :] = from_[pl.ds(idx_ref[base + r], 1), :]

    @pl.loop(1, GC + 1)
    def _(d):
        g = lax.rem(c + d, GC)
        gather(asked, g * 1024, SLOT, src, part)
        packed = jnp.concatenate([part[pl.ds(0, half), :], part[pl.ds(half, half), :]], axis=1).astype(BF16)

        @pl.when(d < GC)
        def _():
            snd[g] = packed
            to(g, d - 1).start()

        @pl.when(d == GC)
        def _():
            rcv[c] = packed

    @pl.loop(0, GC)
    def _(d):
        s = lax.rem(c + GC - d, GC)

        @pl.when(d > 0)
        def _():
            ref = rcv.at[s]
            pltpu.make_async_copy(ref, ref, recv_sem.at[d - 1]).wait()

        got = rcv[s].astype(F32)
        src[pl.ds(pl.multiple_of(s * SLOT, SLOT), half), :] = got[:, :OUTF]
        src[pl.ds(pl.multiple_of(s * SLOT + half, half), half), :] = got[:, OUTF:]

    gather(take, 0, PTS, src, res)
    out[...] = res[...].T.astype(BF16)

    @pl.loop(1, GC)
    def _(d):
        to(lax.rem(c + d, GC), d - 1).wait_send()


def grid_call(rows, asked, take):
    vmem = pl.BlockSpec(memory_space=pltpu.VMEM)
    any_ = pl.BlockSpec(memory_space=pl.ANY)
    dma = pltpu.SemaphoreType.DMA
    return pl.pallas_call(
        grid_kernel,
        out_shape=jax.ShapeDtypeStruct((OUTF, PTS), BF16),
        in_specs=[vmem, any_, any_],
        out_specs=vmem,
        scratch_shapes=[
            pltpu.SMEM(asked.shape, jnp.int32),
            pltpu.SMEM(take.shape, jnp.int32),
            pltpu.VMEM((PTS, OUTF), F32),
            pltpu.VMEM((SLOT, OUTF), F32),
            pltpu.VMEM((GC, SLOT // 2, 2 * OUTF), BF16),
            pltpu.VMEM((GC, SLOT // 2, 2 * OUTF), BF16),
            pltpu.VMEM((PTS, OUTF), F32),
            dma((GC - 1,)), dma((GC - 1,)), dma((2,)),
        ],
        compiler_params=pltpu.CompilerParams(
            collective_id=1, has_side_effects=True, vmem_limit_bytes=40 * 1024 * 1024),
        name="grid_rows",
    )(rows, asked, take)


def local(gaussian, left_basis, right_basis, tile_ranks, diag_factor, morton_of_grid):
    zt = gaussian.T.reshape(2, HALF, NK * CHUNK)
    morton = morton_of_grid.reshape(PTS // 128, 128)
    rows, asked, take = sums_call(zt, left_basis, right_basis, tile_ranks, diag_factor, morton)
    return grid_call(rows, asked.reshape(GC * 1024), take.reshape(PTS)).T


def solution(mesh):
    placed = (
        P("trow", "tcol"),
        P("tcol", "trow", None, None),
        P("tcol", "trow", None, None),
        P("tcol", "trow"),
        P("tcol", "trow", None),
        P("tcol"),
    )
    return jax.shard_map(
        local, mesh=mesh, in_specs=placed, out_specs=P("tcol", "trow"), check_vma=False
    )
```

```python
import jax
import jax.numpy as jnp
from jax import lax
from jax.experimental import pallas as pl
from jax.experimental.pallas import tpu as pltpu
from jax.sharding import PartitionSpec as P

MESH = pl.DeviceIdType.MESH
F32 = jnp.float32
BF16 = jnp.bfloat16
TILE = 2048
RANK = 128
FIELDS = 512
NK = 3
GC = 16
GT = 8
MINE = FIELDS // GC
HALF = MINE // 2
ALL = FIELDS // 2
OUTF = FIELDS // GT
CHUNK = 2 * TILE
BAND = TILE // GT
PART = TILE // 4
PTS = NK * TILE
SLOT = PTS // GC


def place():
    t = lax.axis_index("trow")
    c = lax.axis_index("tcol")
    return t, c


def sums_kernel(
    zt, left, right, ranks, diag, morton,
    out, asked, take,
    zf, pt, b0, b1, b2, a0, a1, a2, r0, r1, r2, snd, rcv, zq, zi, dg, wanted,
    g_send, g_recv, d_send, d_recv, q_send, q_recv, i_send, i_recv, y_send, y_recv, s_send, s_recv, l_send, l_recv,
    loc_r, loc_b, loc_z, loc_d, loc_l, loc_q,
):
    t, c = place()
    z, yl = t // 2, t % 2
    x, yh, core = c // 4, (c // 2) % 2, c % 2
    bs = (b0, b1, b2)
    as_ = (a0, a1, a2)
    rs = (r0, r1, r2)

    def cat(xx, yy, cc):
        return lax.rem(xx + 4, 4) * 4 + yy * 2 + cc

    def tat(zz, yy):
        return lax.rem(zz + 4, 4) * 2 + yy

    barrier = pltpu.get_barrier_semaphore()
    for d in range(1, GT):
        pl.semaphore_signal(barrier, inc=1, device_id=(lax.rem(t + d, GT), c), device_id_type=MESH)
    for d in range(1, GC):
        pl.semaphore_signal(barrier, inc=1, device_id=(t, lax.rem(c + d, GC)), device_id_type=MESH)
    pl.semaphore_wait(barrier, GT - 1 + GC - 1)

    def block(e, cc):
        rows = pl.ds(pl.multiple_of(cc * HALF, HALF), HALF)
        return zf.at[e, :, rows, :] if e < 2 else zf.at[2, e - 2, rows, :]

    def mine(e):
        cols = pl.ds(min(e, 2) * CHUNK, CHUNK)
        return zt.at[:, :, cols] if e < 2 else zt.at[e - 2, :, cols]

    def remote(src, dst, ssem, rsem, dev):
        return pltpu.make_async_remote_copy(
            src_ref=src, dst_ref=dst, send_sem=ssem, recv_sem=rsem, device_id=dev, device_id_type=MESH)

    sent = []

    def go(cp):
        cp.start()
        sent.append(cp)

    def drain(upto):
        for cp in sent[:upto]:
            cp.wait_send()
        del sent[:upto]

    xp = (t, cat(x + 1, yh, core))
    xm = (t, cat(x - 1, yh, core))
    yp = (t, cat(x, 1 - yh, core))
    sib = (t, cat(x, yh, 1 - core))
    zp = (tat(z + 1, yl), c)
    zm = (tat(z - 1, yl), c)
    ylp = (tat(z, 1 - yl), c)

    def slot_block(i, cc):
        return (
            cat(x, 1 - yh, cc), cat(x - 1, yh, cc), cat(x + 1, yh, cc), cat(x - 1, 1 - yh, cc),
            cat(x + 1, 1 - yh, cc), cat(x - 2, yh, cc), cat(x + 2, 1 - yh, cc))[i]

    def fwd(k, i_block, src, i_send, slot, dev):
        go(remote(src, block(k, i_block), g_send.at[k, i_send], g_recv.at[k, slot], dev))

    def got(k, slot, cc):
        ref = block(k, cc)
        pltpu.make_async_copy(ref, ref, g_recv.at[k, slot]).wait()

    def gather_a(k):
        src = mine(k)
        fwd(k, c, src, 0, 0, yp)
        fwd(k, c, src, 2, 2, xm)

    def gather_e(k):
        src = mine(k)
        fwd(k, c, src, 1, 1, xp)
        fwd(k, c, src, 7, 7, sib)

    def relay(k, i, targets):
        cc = slot_block(i, core)
        got(k, i, cc)
        for i_send, slot, dev in targets:
            fwd(k, cc, block(k, cc), i_send, slot, dev)
        fwd(k, cc, block(k, cc), 8 + i, 8 + i, sib)

    def gather_b(k):
        relay(k, 0, ((3, 3, xp), (4, 4, xm)))
        if k < 3:
            relay(k, 1, ())
            relay(k, 2, ())
            far = cat(x - 1 + 2 * core, yh, core)
            fwd(k, far, block(k, far), 5, 5, (t, cat(x + 1 - 2 * core, yh, core)))
        else:
            relay(k, 1, ((5, 5, xp),))
            relay(k, 2, ())

    def gather_d(k):
        got(k, 7, cat(x, yh, 1 - core))
        for i in range(7):
            got(k, 8 + i, slot_block(i, 1 - core))

    def diag_cols(k, zz):
        return diag.at[k, :, pl.ds(pl.multiple_of(zz * PART, PART), PART)]

    def diag_rows(k, zz):
        return dg.at[k, pl.ds(pl.multiple_of(zz * BAND, BAND), BAND), :]

    def diag_send(k):
        for dz in (1, 3, 2):
            zz = lax.rem(z + dz, 4)
            go(remote(diag_cols(k, zz), diag_rows(k, z), d_send.at[k, dz - 1], d_recv.at[k, dz - 1], (tat(zz, yl), c)))

    def diag_wait(k):
        for dz in range(1, 4):
            ref = diag_rows(k, lax.rem(z + 4 - dz, 4))
            pltpu.make_async_copy(ref, ref, d_recv.at[k, dz - 1]).wait()

    def zi_from(k, h, zz):
        return zt.at[:, :, pl.ds(pl.multiple_of((2 * k + h) * TILE + zz * PART, PART), PART)]

    def zi_at(k, h, zz):
        return zq.at[zz, :, :, pl.ds((h * NK + k) * PART, PART)]

    def zi_first():
        for k in range(NK):
            for h in range(2):
                i = h * NK + k
                pltpu.make_async_copy(zi_from(k, h, z), zi_at(k, h, z), loc_q.at[i]).start()
                for dz in (1, 3, 2):
                    zz = lax.rem(z + dz, 4)
                    go(remote(zi_from(k, h, zz), zi_at(k, h, z), q_send.at[dz - 1, i], q_recv.at[dz - 1, i],
                              (tat(zz, yl), c)))

    def zi_piece(g):
        return zq.at[(g % GT) // 2, :, :, pl.ds(pl.multiple_of(g // GT * NK * PART, NK * PART), NK * PART)]

    def zi_rows(cc):
        return zi.at[:, pl.ds(pl.multiple_of(cc * HALF, HALF), HALF), :]

    def zi_remote(d):
        g = lax.rem(2 * (c // 2) + 2 * d, GC) + yl
        return remote(zi_piece(g), zi_rows(c), i_send.at[d], i_recv.at[c], (t, g))

    def zi_second():
        for k in range(NK):
            for h in range(2):
                i = h * NK + k
                pltpu.make_async_copy(zi_from(k, h, z), zi_at(k, h, z), loc_q.at[i]).wait()
                for dz in range(1, 4):
                    ref = zi_at(k, h, lax.rem(z + 4 - dz, 4))
                    pltpu.make_async_copy(ref, ref, q_recv.at[dz - 1, i]).wait()
        for d in range(1, GC // 2):
            go(zi_remote(d))

        @pl.when(core != yl)
        def _():
            zi_remote(0).start()

        @pl.when(core == yl)
        def _():
            pltpu.make_async_copy(zi_piece(c), zi_rows(c), i_recv.at[c]).start()

    def zi_cols(k):
        return zi.at[:, :, pl.ds(k * PART, PART)]

    def zi_pass(k):
        return remote(zi_cols(k), zi_cols(k), y_send.at[k], y_recv.at[k], ylp)

    def zi_third():
        @pl.when(core == yl)
        def _():
            @pl.loop(0, GC)
            def _(cc):
                pltpu.make_async_copy(zi_rows(cc), zi_rows(cc), i_recv.at[cc]).wait()

            zi_pass(0).start()

    def zi_more(k):
        @pl.when(core == yl)
        def _():
            zi_pass(k).start()

    def zi_wait(k):
        @pl.when(core != yl)
        def _():
            pltpu.make_async_copy(zi_cols(k), zi_cols(k), y_recv.at[k]).wait()

    def zi_sent():
        @pl.when(core != yl)
        def _():
            zi_remote(0).wait_send()

        @pl.when(core == yl)
        def _():
            for k in range(NK):
                zi_pass(k).wait_send()

    def right_copies(k):
        return [
            pltpu.make_async_copy(right.at[kk, 2 * k + jj], rs[k].at[jj, :, pl.ds((kk - k) * RANK, RANK)],
                                  loc_r.at[k, jj * NK + kk])
            for jj in range(2) for kk in range(k, NK)]

    def left_copies(k):
        return [
            pltpu.make_async_copy(left.at[k, j], bs[k].at[:, pl.ds(j * RANK, RANK)], loc_b.at[k, j])
            for j in range(2 * k + 2)]

    def z_copy(k):
        rows = pl.ds(pl.multiple_of(c * HALF, HALF), HALF)
        return pltpu.make_async_copy(zt.at[:, :, pl.ds(k * CHUNK, CHUNK)], zf.at[k, :, rows, :], loc_z.at[k])

    def d_copy(k):
        return pltpu.make_async_copy(diag_cols(k, z), diag_rows(k, z), loc_d.at[k])

    def coeffs(k, h=None):
        if h != 1:
            for cp in right_copies(k):
                cp.wait()
            z_copy(k).wait()
        n = NK - k
        lane = lax.broadcasted_iota(jnp.int32, (1, RANK), 1)
        for jj in range(2):
            def one(m):
                rows = pl.ds(m * ALL, ALL)
                acc = jnp.dot(zf[k, m, :, pl.ds(jj * TILE, TILE)], rs[k][jj], preferred_element_type=F32)
                for i in range(n):
                    keep = lane < ranks[k + i, 2 * k + jj]
                    part = jnp.where(keep, acc[:, i * RANK:(i + 1) * RANK], 0.0)
                    as_[k + i][rows, pl.ds((2 * k + jj) * RANK, RANK)] = part.astype(BF16)

            for m in range(2) if h is None else (h,):
                one(m)

    def partial(k, h=None):
        if h != 1:
            for cp in left_copies(k):
                cp.wait()
            d_copy(k).wait()
            diag_wait(k)
            zi_wait(k)
        halves = range(2) if h is None else (h,)

        @pl.loop(0, 4)
        def _(n):
            here = pl.ds(pl.multiple_of((2 * n + yl) * BAND, BAND), BAND)
            other = pl.ds(pl.multiple_of((2 * n + 1 - yl) * BAND, BAND), BAND)
            rows = pl.ds(pl.multiple_of(n * BAND, BAND), BAND)
            for m in halves:
                a = as_[k][pl.ds(m * ALL, ALL), :]
                pt[k % 2, m, :, other] = lax.dot_general(
                    a, bs[k][other, :], (((1,), (1,)), ((), ())), preferred_element_type=F32)
                pt[k % 2, m, :, here] = lax.dot_general(
                    a, bs[k][here, :], (((1,), (1,)), ((), ())), preferred_element_type=F32
                ) + lax.dot_general(
                    zi[m, :, pl.ds(k * PART, PART)], dg[k, rows, :], (((1,), (1,)), ((), ())),
                    preferred_element_type=F32)

    def held(e, zz, side):
        rows = pl.ds(pl.multiple_of((lax.rem(zz + 4, 4) * 2 + side) * MINE, MINE), MINE)
        return pt.at[e % 2, :, rows, :] if e < 2 else pt.at[0, e - 2, rows, :]

    def box(buf, e, i):
        return buf.at[e, i] if e < 2 else buf.at[2, i, e - 2]

    def ship(e, i, value, dev):
        ref = box(snd, e, i)
        ref[...] = value.astype(BF16)
        go(remote(ref, box(rcv, e, i), s_send.at[e, i], s_recv.at[e, i], dev))

    def landed(e, i):
        ref = box(rcv, e, i)
        pltpu.make_async_copy(ref, ref, s_recv.at[e, i]).wait()
        return ref[...].astype(F32)

    def sums_a(e):
        ship(e, 0, held(e, z + 2, 0)[...], zp)
        ship(e, 1, held(e, z + 2, 1)[...], zm)
        ship(e, 2, held(e, z + 1, 1)[...], zp)
        ship(e, 3, held(e, z - 1, 0)[...], zm)

    def sums_b(e):
        ship(e, 4, held(e, z + 1, 0)[...] + landed(e, 0), zp)
        ship(e, 5, held(e, z - 1, 1)[...] + landed(e, 1), zm)

    def sums_c(e):
        held(e, z, 1)[...] += landed(e, 2)
        held(e, z, 0)[...] += landed(e, 3)
        held(e, z, 0)[...] += landed(e, 4)
        held(e, z, 1)[...] += landed(e, 5)
        ship(e, 6, held(e, z, 1 - yl)[...], ylp)

    def sums_d(e):
        total = (held(e, z, yl)[...] + landed(e, 6)).astype(BF16)
        cols = pl.ds(min(e, 2) * TILE, TILE)
        for q in range(2):
            if e < 2:
                for h in range(2):
                    out[pl.ds(q * MINE + h * HALF, HALF), cols] = total[h, q * HALF:(q + 1) * HALF]
            else:
                out[pl.ds(q * MINE + (e - 2) * HALF, HALF), cols] = total[q * HALF:(q + 1) * HALF]

    def lists():
        m = morton[...]
        tile = m // TILE
        source = tile % GC
        row = tile // GC * TILE + m % TILE
        lane = lax.broadcasted_iota(jnp.int32, (128, 128), 1)
        before = (lax.broadcasted_iota(jnp.int32, (128, 128), 0) < lane).astype(BF16)
        n = PTS // 128
        above = (lax.broadcasted_iota(jnp.int32, (n, n), 1) < lax.broadcasted_iota(jnp.int32, (n, n), 0)).astype(BF16)
        rank = jnp.zeros((n, 128), F32)
        for g in range(GC):
            one = (source == g).astype(F32)
            ones = one.astype(BF16)
            inside = jnp.dot(ones, before, preferred_element_type=F32)
            ahead = jnp.sum(jnp.dot(above, ones, preferred_element_type=F32), axis=1, keepdims=True)
            rank = rank + one * (inside + ahead)
        rank = rank.astype(jnp.int32)
        take[...] = source * SLOT + rank
        group = lax.broadcasted_iota(jnp.int32, (GC, 128), 0)
        spot = lax.broadcasted_iota(jnp.int32, (SLOT, 128), 0)
        both = jnp.zeros((2 * GC, SLOT), F32)
        for i in range(n):
            at = (spot == rank[i:i + 1]).astype(F32).astype(BF16)
            here = group == source[i:i + 1]
            high = jnp.where(here, row[i:i + 1] // 128, 0)
            low = jnp.where(here, row[i:i + 1] % 128, 0)
            pair = jnp.concatenate([high, low], axis=0).astype(F32).astype(BF16)
            both = both + lax.dot_general(pair, at, (((1,), (1,)), ((), ())), preferred_element_type=F32)
        both = both.astype(jnp.int32)
        rows = both[:GC] * 128 + both[GC:]
        wanted[...] = jnp.zeros_like(wanted)
        for q in range(SLOT // 128):
            wanted[:, q, :] = rows[:, q * 128:(q + 1) * 128]

    def list_send():
        for d in range(1, GC):
            g = lax.rem(c + d, GC)
            go(remote(wanted.at[g], asked.at[c], l_send.at[d - 1], l_recv.at[d - 1], (t, g)))

    gather_a(0)
    gather_e(0)
    zi_first()
    diag_send(0)
    z_copy(0).start()
    for cp in right_copies(0):
        cp.start()
    gather_b(0)
    zi_second()
    gather_a(1)
    relay(0, 3, ())
    gather_e(1)
    relay(0, 4, ())
    diag_send(1)
    for k in range(NK):
        d_copy(k).start()
        for cp in left_copies(k):
            cp.start()
        if k:
            z_copy(k).start()
            for cp in right_copies(k):
                cp.start()
    zi_third()
    relay(0, 5, ((6, 6, yp),))
    relay(0, 6, ())
    lists()
    own_list = pltpu.make_async_copy(wanted.at[c], asked.at[c], loc_l)
    own_list.start()
    list_send()
    gather_d(0)
    coeffs(0)
    gather_b(1)
    gather_a(2)
    diag_send(2)
    relay(1, 3, ())
    gather_e(2)
    relay(1, 4, ())
    partial(0)
    sums_a(0)
    zi_more(1)
    relay(1, 5, ((6, 6, yp),))
    relay(1, 6, ())
    gather_d(1)
    sums_b(0)
    old = len(sent)
    coeffs(1)
    gather_b(2)
    gather_a(3)
    zi_more(2)
    partial(1)
    sums_a(1)
    relay(2, 3, ())
    gather_e(3)
    relay(2, 4, ())
    sums_c(0)
    relay(2, 5, ((6, 6, yp),))
    relay(2, 6, ())
    gather_d(2)
    coeffs(2, 0)
    gather_b(3)
    sums_b(1)
    sums_d(0)
    partial(2, 0)
    sums_a(2)
    relay(3, 3, ())
    relay(3, 4, ((6, 6, xm),))
    relay(3, 5, ())
    relay(3, 6, ())
    sums_c(1)
    drain(old)
    own_list.wait()
    for d in range(1, GC):
        ref = asked.at[lax.rem(c + GC - d, GC)]
        pltpu.make_async_copy(ref, ref, l_recv.at[d - 1]).wait()
    zi_sent()
    newer = len(sent)
    gather_d(3)
    coeffs(2, 1)
    partial(2, 1)
    sums_a(3)
    sums_b(2)
    sums_d(1)
    drain(newer)
    sums_b(3)
    sums_c(2)
    sums_c(3)
    sums_d(2)
    sums_d(3)
    drain(len(sent))


def sums_call(zt, left, right, ranks, diag, morton):
    any_ = pl.BlockSpec(memory_space=pl.ANY)
    vmem = pl.BlockSpec(memory_space=pltpu.VMEM)
    dma = pltpu.SemaphoreType.DMA
    return pl.pallas_call(
        sums_kernel,
        out_shape=(
            jax.ShapeDtypeStruct((OUTF, PTS), BF16),
            jax.ShapeDtypeStruct((GC, 8, 128), jnp.int32),
            jax.ShapeDtypeStruct((PTS // 128, 128), jnp.int32),
        ),
        in_specs=[any_, any_, any_, pl.BlockSpec(memory_space=pltpu.SMEM), any_, vmem],
        out_specs=(vmem, any_, vmem),
        scratch_shapes=[
            pltpu.VMEM((NK, 2, ALL, CHUNK), BF16),
            pltpu.VMEM((2, 2, ALL, TILE), F32),
            *[pltpu.VMEM((TILE, 2 * RANK * (k + 1)), BF16) for k in range(NK)],
            *[pltpu.VMEM((FIELDS, 2 * RANK * (k + 1)), BF16) for k in range(NK)],
            *[pltpu.VMEM((2, TILE, RANK * (NK - k)), BF16) for k in range(NK)],
            pltpu.VMEM((NK, 7, 2, MINE, TILE), BF16),
            pltpu.VMEM((NK, 7, 2, MINE, TILE), BF16),
            pltpu.VMEM((4, 2, HALF, 2 * NK * PART), BF16),
            pltpu.VMEM((2, ALL, NK * PART), BF16),
            pltpu.VMEM((NK, 4 * BAND, PART), BF16),
            pltpu.VMEM((GC, 8, 128), jnp.int32),
            dma((4, 15)), dma((4, 15)), dma((NK, 3)), dma((NK, 3)),
            dma((3, 2 * NK)), dma((3, 2 * NK)), dma((GC // 2,)), dma((GC,)), dma((NK,)), dma((NK,)),
            dma((4, 7)), dma((4, 7)), dma((GC - 1,)), dma((GC - 1,)),
            dma((NK, 2 * NK)), dma((NK, 2 * NK)), dma((NK,)), dma((NK,)), dma, dma((2 * NK,)),
        ],
        compiler_params=pltpu.CompilerParams(
            collective_id=0, has_side_effects=True, vmem_limit_bytes=60 * 1024 * 1024),
        cost_estimate=pl.CostEstimate(flops=17_000_000_000, bytes_accessed=20_000_000, transcendentals=0),
        name="tile_sums",
    )(zt, left, right, ranks, diag, morton)


def grid_kernel(rows_in, asked_in, take_in, out, rows, asked, take, src, part, snd, rcv, res, send_sem, recv_sem, loc):
    t, c = place()
    barrier = pltpu.get_barrier_semaphore()
    for d in range(1, GC):
        pl.semaphore_signal(barrier, inc=1, device_id=(t, lax.rem(c + d, GC)), device_id_type=MESH)
    half = SLOT // 2
    fetch_asked = pltpu.make_async_copy(asked_in, asked, loc.at[0])
    fetch_asked.start()
    fetch_take = pltpu.make_async_copy(take_in, take, loc.at[1])
    fetch_take.start()
    fetch_rows = pltpu.make_async_copy(rows_in, rows, loc.at[2])
    fetch_rows.start()
    fetch_rows.wait()
    src[...] = rows[...].astype(F32).T
    fetch_asked.wait()
    fetch_take.wait()
    pl.semaphore_wait(barrier, GC - 1)

    def to(g, d):
        return pltpu.make_async_remote_copy(
            src_ref=snd.at[g], dst_ref=rcv.at[c], send_sem=send_sem.at[d], recv_sem=recv_sem.at[d],
            device_id=(t, g), device_id_type=MESH)

    def gather(idx_ref, base, n, from_, to_):
        @pl.loop(0, n // 16)
        def _(i):
            for u in range(16):
                r = i * 16 + u
                to_[pl.ds(r, 1), :] = from_[pl.ds(idx_ref[base + r], 1), :]

    @pl.loop(1, GC + 1)
    def _(d):
        g = lax.rem(c + d, GC)
        gather(asked, g * 1024, SLOT, src, part)
        packed = jnp.concatenate([part[pl.ds(0, half), :], part[pl.ds(half, half), :]], axis=1).astype(BF16)

        @pl.when(d < GC)
        def _():
            snd[g] = packed
            to(g, d - 1).start()

        @pl.when(d == GC)
        def _():
            rcv[c] = packed

    @pl.loop(0, GC)
    def _(d):
        s = lax.rem(c + GC - d, GC)

        @pl.when(d > 0)
        def _():
            ref = rcv.at[s]
            pltpu.make_async_copy(ref, ref, recv_sem.at[d - 1]).wait()

        got = rcv[s].astype(F32)
        src[pl.ds(pl.multiple_of(s * SLOT, SLOT), half), :] = got[:, :OUTF]
        src[pl.ds(pl.multiple_of(s * SLOT + half, half), half), :] = got[:, OUTF:]

    gather(take, 0, PTS, src, res)
    out[...] = res[...].T.astype(BF16)

    @pl.loop(1, GC)
    def _(d):
        to(lax.rem(c + d, GC), d - 1).wait_send()


def grid_call(rows, asked, take):
    vmem = pl.BlockSpec(memory_space=pltpu.VMEM)
    any_ = pl.BlockSpec(memory_space=pl.ANY)
    dma = pltpu.SemaphoreType.DMA
    return pl.pallas_call(
        grid_kernel,
        out_shape=jax.ShapeDtypeStruct((OUTF, PTS), BF16),
        in_specs=[any_, any_, any_],
        out_specs=vmem,
        scratch_shapes=[
            pltpu.VMEM(rows.shape, BF16),
            pltpu.SMEM(asked.shape, jnp.int32),
            pltpu.SMEM(take.shape, jnp.int32),
            pltpu.VMEM((PTS, OUTF), F32),
            pltpu.VMEM((SLOT, OUTF), F32),
            pltpu.VMEM((GC, SLOT // 2, 2 * OUTF), BF16),
            pltpu.VMEM((GC, SLOT // 2, 2 * OUTF), BF16),
            pltpu.VMEM((PTS, OUTF), F32),
            dma((GC - 1,)), dma((GC - 1,)), dma((3,)),
        ],
        compiler_params=pltpu.CompilerParams(
            collective_id=1, has_side_effects=True, vmem_limit_bytes=60 * 1024 * 1024),
        name="grid_rows",
    )(rows, asked, take)


def local(gaussian, left_basis, right_basis, tile_ranks, diag_factor, morton_of_grid):
    zt = gaussian.T.reshape(2, HALF, NK * CHUNK)
    morton = morton_of_grid.reshape(PTS // 128, 128)
    rows, asked, take = sums_call(zt, left_basis, right_basis, tile_ranks, diag_factor, morton)
    return grid_call(rows, asked.reshape(GC * 1024), take.reshape(PTS)).T


def solution(mesh):
    placed = (
        P("trow", "tcol"),
        P("tcol", "trow", None, None),
        P("tcol", "trow", None, None),
        P("tcol", "trow"),
        P("tcol", "trow", None),
        P("tcol"),
    )
    return jax.shard_map(
        local, mesh=mesh, in_specs=placed, out_specs=P("tcol", "trow"), check_vma=False
    )
```

```python
import jax
import jax.numpy as jnp
from jax import lax
from jax.experimental import pallas as pl
from jax.experimental.pallas import tpu as pltpu
from jax.sharding import PartitionSpec as P

MESH = pl.DeviceIdType.MESH
F32 = jnp.float32
BF16 = jnp.bfloat16
TILE = 2048
RANK = 128
FIELDS = 512
NK = 3
GC = 16
GT = 8
MINE = FIELDS // GC
HALF = MINE // 2
ALL = FIELDS // 2
OUTF = FIELDS // GT
CHUNK = 2 * TILE
BAND = TILE // GT
PART = TILE // 4
PTS = NK * TILE
SLOT = PTS // GC


def place():
    t = lax.axis_index("trow")
    c = lax.axis_index("tcol")
    return t, c


def sums_kernel(
    zt, left, right, ranks, diag, morton,
    out, asked, take,
    zf, pt, b0, b1, b2, a0, a1, a2, r0, r1, r2, snd, rcv, zq, zi, dg, wanted,
    g_send, g_recv, d_send, d_recv, q_send, q_recv, i_send, i_recv, y_send, y_recv, s_send, s_recv, l_send, l_recv,
    loc_r, loc_b, loc_z, loc_d, loc_l, loc_q,
):
    t, c = place()
    z, yl = t // 2, t % 2
    x, yh, core = c // 4, (c // 2) % 2, c % 2
    bs = (b0, b1, b2)
    as_ = (a0, a1, a2)
    rs = (r0, r1, r2)

    def cat(xx, yy, cc):
        return lax.rem(xx + 4, 4) * 4 + yy * 2 + cc

    def tat(zz, yy):
        return lax.rem(zz + 4, 4) * 2 + yy

    barrier = pltpu.get_barrier_semaphore()
    for d in range(1, GT):
        pl.semaphore_signal(barrier, inc=1, device_id=(lax.rem(t + d, GT), c), device_id_type=MESH)
    for d in range(1, GC):
        pl.semaphore_signal(barrier, inc=1, device_id=(t, lax.rem(c + d, GC)), device_id_type=MESH)
    pl.semaphore_wait(barrier, GT - 1 + GC - 1)

    def block(e, cc):
        rows = pl.ds(pl.multiple_of(cc * HALF, HALF), HALF)
        return zf.at[e, :, rows, :] if e < 2 else zf.at[2, e - 2, rows, :]

    def mine(e):
        cols = pl.ds(min(e, 2) * CHUNK, CHUNK)
        return zt.at[:, :, cols] if e < 2 else zt.at[e - 2, :, cols]

    def remote(src, dst, ssem, rsem, dev):
        return pltpu.make_async_remote_copy(
            src_ref=src, dst_ref=dst, send_sem=ssem, recv_sem=rsem, device_id=dev, device_id_type=MESH)

    sent = []

    def go(cp):
        cp.start()
        sent.append(cp)

    def drain(upto):
        for cp in sent[:upto]:
            cp.wait_send()
        del sent[:upto]

    xp = (t, cat(x + 1, yh, core))
    xm = (t, cat(x - 1, yh, core))
    yp = (t, cat(x, 1 - yh, core))
    sib = (t, cat(x, yh, 1 - core))
    zp = (tat(z + 1, yl), c)
    zm = (tat(z - 1, yl), c)
    ylp = (tat(z, 1 - yl), c)

    def slot_block(i, cc):
        return (
            cat(x, 1 - yh, cc), cat(x - 1, yh, cc), cat(x + 1, yh, cc), cat(x - 1, 1 - yh, cc),
            cat(x + 1, 1 - yh, cc), cat(x - 2, yh, cc), cat(x + 2, 1 - yh, cc))[i]

    def fwd(k, i_block, src, i_send, slot, dev):
        go(remote(src, block(k, i_block), g_send.at[k, i_send], g_recv.at[k, slot], dev))

    def got(k, slot, cc):
        ref = block(k, cc)
        pltpu.make_async_copy(ref, ref, g_recv.at[k, slot]).wait()

    def gather_a(k):
        src = mine(k)
        fwd(k, c, src, 0, 0, yp)
        fwd(k, c, src, 2, 2, xm)

    def gather_e(k):
        src = mine(k)
        fwd(k, c, src, 1, 1, xp)
        fwd(k, c, src, 7, 7, sib)

    def relay(k, i, targets):
        cc = slot_block(i, core)
        got(k, i, cc)
        for i_send, slot, dev in targets:
            fwd(k, cc, block(k, cc), i_send, slot, dev)
        fwd(k, cc, block(k, cc), 8 + i, 8 + i, sib)

    def gather_b(k):
        relay(k, 0, ((3, 3, xp), (4, 4, xm)))
        relay(k, 1, ((5, 5, xp),))
        relay(k, 2, ())

    def gather_d(k):
        got(k, 7, cat(x, yh, 1 - core))
        for i in range(7):
            got(k, 8 + i, slot_block(i, 1 - core))

    def diag_cols(k, zz):
        return diag.at[k, :, pl.ds(pl.multiple_of(zz * PART, PART), PART)]

    def diag_rows(k, zz):
        return dg.at[k, pl.ds(pl.multiple_of(zz * BAND, BAND), BAND), :]

    def diag_send(k):
        for dz in (1, 3, 2):
            zz = lax.rem(z + dz, 4)
            go(remote(diag_cols(k, zz), diag_rows(k, z), d_send.at[k, dz - 1], d_recv.at[k, dz - 1], (tat(zz, yl), c)))

    def diag_wait(k):
        for dz in range(1, 4):
            ref = diag_rows(k, lax.rem(z + 4 - dz, 4))
            pltpu.make_async_copy(ref, ref, d_recv.at[k, dz - 1]).wait()

    def zi_from(k, h, zz):
        return zt.at[:, :, pl.ds(pl.multiple_of((2 * k + h) * TILE + zz * PART, PART), PART)]

    def zi_at(k, h, zz):
        return zq.at[zz, :, :, pl.ds((h * NK + k) * PART, PART)]

    def zi_first():
        for k in range(NK):
            for h in range(2):
                i = h * NK + k
                pltpu.make_async_copy(zi_from(k, h, z), zi_at(k, h, z), loc_q.at[i]).start()
                for dz in (1, 3, 2):
                    zz = lax.rem(z + dz, 4)
                    go(remote(zi_from(k, h, zz), zi_at(k, h, z), q_send.at[dz - 1, i], q_recv.at[dz - 1, i],
                              (tat(zz, yl), c)))

    def zi_piece(g):
        return zq.at[(g % GT) // 2, :, :, pl.ds(pl.multiple_of(g // GT * NK * PART, NK * PART), NK * PART)]

    def zi_rows(cc):
        return zi.at[:, pl.ds(pl.multiple_of(cc * HALF, HALF), HALF), :]

    def zi_remote(d):
        g = lax.rem(2 * (c // 2) + 2 * d, GC) + yl
        return remote(zi_piece(g), zi_rows(c), i_send.at[d], i_recv.at[c], (t, g))

    def zi_second():
        for k in range(NK):
            for h in range(2):
                i = h * NK + k
                pltpu.make_async_copy(zi_from(k, h, z), zi_at(k, h, z), loc_q.at[i]).wait()
                for dz in range(1, 4):
                    ref = zi_at(k, h, lax.rem(z + 4 - dz, 4))
                    pltpu.make_async_copy(ref, ref, q_recv.at[dz - 1, i]).wait()
        for d in range(1, GC // 2):
            go(zi_remote(d))

        @pl.when(core != yl)
        def _():
            zi_remote(0).start()

        @pl.when(core == yl)
        def _():
            pltpu.make_async_copy(zi_piece(c), zi_rows(c), i_recv.at[c]).start()

    def zi_cols(k):
        return zi.at[:, :, pl.ds(k * PART, PART)]

    def zi_pass(k):
        return remote(zi_cols(k), zi_cols(k), y_send.at[k], y_recv.at[k], ylp)

    def zi_third():
        @pl.when(core == yl)
        def _():
            @pl.loop(0, GC)
            def _(cc):
                pltpu.make_async_copy(zi_rows(cc), zi_rows(cc), i_recv.at[cc]).wait()

            zi_pass(0).start()

    def zi_more(k):
        @pl.when(core == yl)
        def _():
            zi_pass(k).start()

    def zi_wait(k):
        @pl.when(core != yl)
        def _():
            pltpu.make_async_copy(zi_cols(k), zi_cols(k), y_recv.at[k]).wait()

    def zi_sent():
        @pl.when(core != yl)
        def _():
            zi_remote(0).wait_send()

        @pl.when(core == yl)
        def _():
            for k in range(NK):
                zi_pass(k).wait_send()

    def right_copies(k):
        return [
            pltpu.make_async_copy(right.at[kk, 2 * k + jj], rs[k].at[jj, :, pl.ds((kk - k) * RANK, RANK)],
                                  loc_r.at[k, jj * NK + kk])
            for jj in range(2) for kk in range(k, NK)]

    def left_copies(k):
        return [
            pltpu.make_async_copy(left.at[k, j], bs[k].at[:, pl.ds(j * RANK, RANK)], loc_b.at[k, j])
            for j in range(2 * k + 2)]

    def z_copy(k):
        rows = pl.ds(pl.multiple_of(c * HALF, HALF), HALF)
        return pltpu.make_async_copy(zt.at[:, :, pl.ds(k * CHUNK, CHUNK)], zf.at[k, :, rows, :], loc_z.at[k])

    def d_copy(k):
        return pltpu.make_async_copy(diag_cols(k, z), diag_rows(k, z), loc_d.at[k])

    def coeffs(k, h=None):
        if h != 1:
            for cp in right_copies(k):
                cp.wait()
            z_copy(k).wait()
        n = NK - k
        lane = lax.broadcasted_iota(jnp.int32, (1, RANK), 1)
        for jj in range(2):
            def one(m):
                rows = pl.ds(m * ALL, ALL)
                acc = jnp.dot(zf[k, m, :, pl.ds(jj * TILE, TILE)], rs[k][jj], preferred_element_type=F32)
                for i in range(n):
                    keep = lane < ranks[k + i, 2 * k + jj]
                    part = jnp.where(keep, acc[:, i * RANK:(i + 1) * RANK], 0.0)
                    as_[k + i][rows, pl.ds((2 * k + jj) * RANK, RANK)] = part.astype(BF16)

            for m in range(2) if h is None else (h,):
                one(m)

    def partial(k, h=None):
        if h != 1:
            for cp in left_copies(k):
                cp.wait()
            d_copy(k).wait()
            diag_wait(k)
            zi_wait(k)
        halves = range(2) if h is None else (h,)

        @pl.loop(0, 4)
        def _(n):
            here = pl.ds(pl.multiple_of((2 * n + yl) * BAND, BAND), BAND)
            other = pl.ds(pl.multiple_of((2 * n + 1 - yl) * BAND, BAND), BAND)
            rows = pl.ds(pl.multiple_of(n * BAND, BAND), BAND)
            for m in halves:
                a = as_[k][pl.ds(m * ALL, ALL), :]
                pt[k % 2, m, :, other] = lax.dot_general(
                    a, bs[k][other, :], (((1,), (1,)), ((), ())), preferred_element_type=F32)
                pt[k % 2, m, :, here] = lax.dot_general(
                    a, bs[k][here, :], (((1,), (1,)), ((), ())), preferred_element_type=F32
                ) + lax.dot_general(
                    zi[m, :, pl.ds(k * PART, PART)], dg[k, rows, :], (((1,), (1,)), ((), ())),
                    preferred_element_type=F32)

    def held(e, zz, side):
        rows = pl.ds(pl.multiple_of((lax.rem(zz + 4, 4) * 2 + side) * MINE, MINE), MINE)
        return pt.at[e % 2, :, rows, :] if e < 2 else pt.at[0, e - 2, rows, :]

    def box(buf, e, i):
        return buf.at[e, i] if e < 2 else buf.at[2, i, e - 2]

    def ship(e, i, value, dev):
        ref = box(snd, e, i)
        ref[...] = value.astype(BF16)
        go(remote(ref, box(rcv, e, i), s_send.at[e, i], s_recv.at[e, i], dev))

    def landed(e, i):
        ref = box(rcv, e, i)
        pltpu.make_async_copy(ref, ref, s_recv.at[e, i]).wait()
        return ref[...].astype(F32)

    def sums_a(e):
        ship(e, 0, held(e, z + 2, 0)[...], zp)
        ship(e, 1, held(e, z + 2, 1)[...], zm)
        ship(e, 2, held(e, z + 1, 1)[...], zp)
        ship(e, 3, held(e, z - 1, 0)[...], zm)

    def sums_b(e):
        ship(e, 4, held(e, z + 1, 0)[...] + landed(e, 0), zp)
        ship(e, 5, held(e, z - 1, 1)[...] + landed(e, 1), zm)

    def sums_c(e):
        held(e, z, 1)[...] += landed(e, 2)
        held(e, z, 0)[...] += landed(e, 3)
        held(e, z, 0)[...] += landed(e, 4)
        held(e, z, 1)[...] += landed(e, 5)
        ship(e, 6, held(e, z, 1 - yl)[...], ylp)

    def sums_d(e):
        total = (held(e, z, yl)[...] + landed(e, 6)).astype(BF16)
        cols = pl.ds(min(e, 2) * TILE, TILE)
        for q in range(2):
            if e < 2:
                for h in range(2):
                    out[pl.ds(q * MINE + h * HALF, HALF), cols] = total[h, q * HALF:(q + 1) * HALF]
            else:
                out[pl.ds(q * MINE + (e - 2) * HALF, HALF), cols] = total[q * HALF:(q + 1) * HALF]

    def lists():
        m = morton[...]
        tile = m // TILE
        source = tile % GC
        row = tile // GC * TILE + m % TILE
        lane = lax.broadcasted_iota(jnp.int32, (128, 128), 1)
        before = (lax.broadcasted_iota(jnp.int32, (128, 128), 0) < lane).astype(BF16)
        n = PTS // 128
        above = (lax.broadcasted_iota(jnp.int32, (n, n), 1) < lax.broadcasted_iota(jnp.int32, (n, n), 0)).astype(BF16)
        rank = jnp.zeros((n, 128), F32)
        for g in range(GC):
            one = (source == g).astype(F32)
            ones = one.astype(BF16)
            inside = jnp.dot(ones, before, preferred_element_type=F32)
            ahead = jnp.sum(jnp.dot(above, ones, preferred_element_type=F32), axis=1, keepdims=True)
            rank = rank + one * (inside + ahead)
        rank = rank.astype(jnp.int32)
        take[...] = source * SLOT + rank
        group = lax.broadcasted_iota(jnp.int32, (GC, 128), 0)
        spot = lax.broadcasted_iota(jnp.int32, (SLOT, 128), 0)
        both = jnp.zeros((2 * GC, SLOT), F32)
        for i in range(n):
            at = (spot == rank[i:i + 1]).astype(F32).astype(BF16)
            here = group == source[i:i + 1]
            high = jnp.where(here, row[i:i + 1] // 128, 0)
            low = jnp.where(here, row[i:i + 1] % 128, 0)
            pair = jnp.concatenate([high, low], axis=0).astype(F32).astype(BF16)
            both = both + lax.dot_general(pair, at, (((1,), (1,)), ((), ())), preferred_element_type=F32)
        both = both.astype(jnp.int32)
        rows = both[:GC] * 128 + both[GC:]
        wanted[...] = jnp.zeros_like(wanted)
        for q in range(SLOT // 128):
            wanted[:, q, :] = rows[:, q * 128:(q + 1) * 128]

    def list_send():
        for d in range(1, GC):
            g = lax.rem(c + d, GC)
            go(remote(wanted.at[g], asked.at[c], l_send.at[d - 1], l_recv.at[d - 1], (t, g)))

    gather_a(0)
    gather_e(0)
    zi_first()
    z_copy(0).start()
    for cp in right_copies(0):
        cp.start()
    gather_b(0)
    diag_send(0)
    gather_a(1)
    relay(0, 3, ())
    gather_e(1)
    relay(0, 4, ((6, 6, xm),))
    zi_second()
    diag_send(1)
    for k in range(NK):
        d_copy(k).start()
        for cp in left_copies(k):
            cp.start()
        if k:
            z_copy(k).start()
            for cp in right_copies(k):
                cp.start()
    relay(0, 5, ())
    relay(0, 6, ())
    lists()
    own_list = pltpu.make_async_copy(wanted.at[c], asked.at[c], loc_l)
    own_list.start()
    list_send()
    gather_d(0)
    coeffs(0)
    zi_third()
    gather_b(1)
    gather_a(2)
    diag_send(2)
    relay(1, 3, ())
    gather_e(2)
    relay(1, 4, ((6, 6, xm),))
    partial(0)
    sums_a(0)
    zi_more(1)
    relay(1, 5, ())
    relay(1, 6, ())
    gather_d(1)
    sums_b(0)
    old = len(sent)
    coeffs(1)
    gather_b(2)
    gather_a(3)
    zi_more(2)
    partial(1)
    sums_a(1)
    relay(2, 3, ())
    gather_e(3)
    relay(2, 4, ((6, 6, xm),))
    sums_c(0)
    relay(2, 5, ())
    relay(2, 6, ())
    gather_d(2)
    coeffs(2, 0)
    gather_b(3)
    sums_b(1)
    sums_d(0)
    partial(2, 0)
    sums_a(2)
    relay(3, 3, ())
    relay(3, 4, ((6, 6, xm),))
    relay(3, 5, ())
    relay(3, 6, ())
    sums_c(1)
    drain(old)
    own_list.wait()
    for d in range(1, GC):
        ref = asked.at[lax.rem(c + GC - d, GC)]
        pltpu.make_async_copy(ref, ref, l_recv.at[d - 1]).wait()
    zi_sent()
    newer = len(sent)
    gather_d(3)
    coeffs(2, 1)
    partial(2, 1)
    sums_a(3)
    sums_b(2)
    sums_d(1)
    drain(newer)
    sums_b(3)
    sums_c(2)
    sums_c(3)
    sums_d(2)
    sums_d(3)
    drain(len(sent))


def sums_call(zt, left, right, ranks, diag, morton):
    any_ = pl.BlockSpec(memory_space=pl.ANY)
    vmem = pl.BlockSpec(memory_space=pltpu.VMEM)
    dma = pltpu.SemaphoreType.DMA
    return pl.pallas_call(
        sums_kernel,
        out_shape=(
            jax.ShapeDtypeStruct((OUTF, PTS), BF16),
            jax.ShapeDtypeStruct((GC, 8, 128), jnp.int32),
            jax.ShapeDtypeStruct((PTS // 128, 128), jnp.int32),
        ),
        in_specs=[any_, any_, any_, pl.BlockSpec(memory_space=pltpu.SMEM), any_, vmem],
        out_specs=(vmem, any_, vmem),
        scratch_shapes=[
            pltpu.VMEM((NK, 2, ALL, CHUNK), BF16),
            pltpu.VMEM((2, 2, ALL, TILE), F32),
            *[pltpu.VMEM((TILE, 2 * RANK * (k + 1)), BF16) for k in range(NK)],
            *[pltpu.VMEM((FIELDS, 2 * RANK * (k + 1)), BF16) for k in range(NK)],
            *[pltpu.VMEM((2, TILE, RANK * (NK - k)), BF16) for k in range(NK)],
            pltpu.VMEM((NK, 7, 2, MINE, TILE), BF16),
            pltpu.VMEM((NK, 7, 2, MINE, TILE), BF16),
            pltpu.VMEM((4, 2, HALF, 2 * NK * PART), BF16),
            pltpu.VMEM((2, ALL, NK * PART), BF16),
            pltpu.VMEM((NK, 4 * BAND, PART), BF16),
            pltpu.VMEM((GC, 8, 128), jnp.int32),
            dma((4, 15)), dma((4, 15)), dma((NK, 3)), dma((NK, 3)),
            dma((3, 2 * NK)), dma((3, 2 * NK)), dma((GC // 2,)), dma((GC,)), dma((NK,)), dma((NK,)),
            dma((4, 7)), dma((4, 7)), dma((GC - 1,)), dma((GC - 1,)),
            dma((NK, 2 * NK)), dma((NK, 2 * NK)), dma((NK,)), dma((NK,)), dma, dma((2 * NK,)),
        ],
        compiler_params=pltpu.CompilerParams(
            collective_id=0, has_side_effects=True, vmem_limit_bytes=60 * 1024 * 1024),
        cost_estimate=pl.CostEstimate(flops=17_000_000_000, bytes_accessed=20_000_000, transcendentals=0),
        name="tile_sums",
    )(zt, left, right, ranks, diag, morton)


def grid_kernel(rows_in, asked_in, take_in, out, rows, asked, take, src, part, snd, rcv, res, send_sem, recv_sem, loc):
    t, c = place()
    barrier = pltpu.get_barrier_semaphore()
    for d in range(1, GC):
        pl.semaphore_signal(barrier, inc=1, device_id=(t, lax.rem(c + d, GC)), device_id_type=MESH)
    half = SLOT // 2
    fetch_asked = pltpu.make_async_copy(asked_in, asked, loc.at[0])
    fetch_asked.start()
    fetch_take = pltpu.make_async_copy(take_in, take, loc.at[1])
    fetch_take.start()
    fetch_rows = pltpu.make_async_copy(rows_in, rows, loc.at[2])
    fetch_rows.start()
    fetch_rows.wait()
    src[...] = rows[...].astype(F32).T
    fetch_asked.wait()
    fetch_take.wait()
    pl.semaphore_wait(barrier, GC - 1)

    def to(g, d):
        return pltpu.make_async_remote_copy(
            src_ref=snd.at[g], dst_ref=rcv.at[c], send_sem=send_sem.at[d], recv_sem=recv_sem.at[d],
            device_id=(t, g), device_id_type=MESH)

    def gather(idx_ref, base, n, from_, to_):
        @pl.loop(0, n // 16)
        def _(i):
            for u in range(16):
                r = i * 16 + u
                to_[pl.ds(r, 1), :] = from_[pl.ds(idx_ref[base + r], 1), :]

    @pl.loop(1, GC + 1)
    def _(d):
        g = lax.rem(c + d, GC)
        gather(asked, g * 1024, SLOT, src, part)
        packed = jnp.concatenate([part[pl.ds(0, half), :], part[pl.ds(half, half), :]], axis=1).astype(BF16)

        @pl.when(d < GC)
        def _():
            snd[g] = packed
            to(g, d - 1).start()

        @pl.when(d == GC)
        def _():
            rcv[c] = packed

    @pl.loop(0, GC)
    def _(d):
        s = lax.rem(c + GC - d, GC)

        @pl.when(d > 0)
        def _():
            ref = rcv.at[s]
            pltpu.make_async_copy(ref, ref, recv_sem.at[d - 1]).wait()

        got = rcv[s].astype(F32)
        src[pl.ds(pl.multiple_of(s * SLOT, SLOT), half), :] = got[:, :OUTF]
        src[pl.ds(pl.multiple_of(s * SLOT + half, half), half), :] = got[:, OUTF:]

    gather(take, 0, PTS, src, res)
    out[...] = res[...].T.astype(BF16)

    @pl.loop(1, GC)
    def _(d):
        to(lax.rem(c + d, GC), d - 1).wait_send()


def grid_call(rows, asked, take):
    vmem = pl.BlockSpec(memory_space=pltpu.VMEM)
    any_ = pl.BlockSpec(memory_space=pl.ANY)
    dma = pltpu.SemaphoreType.DMA
    return pl.pallas_call(
        grid_kernel,
        out_shape=jax.ShapeDtypeStruct((OUTF, PTS), BF16),
        in_specs=[any_, any_, any_],
        out_specs=vmem,
        scratch_shapes=[
            pltpu.VMEM(rows.shape, BF16),
            pltpu.SMEM(asked.shape, jnp.int32),
            pltpu.SMEM(take.shape, jnp.int32),
            pltpu.VMEM((PTS, OUTF), F32),
            pltpu.VMEM((SLOT, OUTF), F32),
            pltpu.VMEM((GC, SLOT // 2, 2 * OUTF), BF16),
            pltpu.VMEM((GC, SLOT // 2, 2 * OUTF), BF16),
            pltpu.VMEM((PTS, OUTF), F32),
            dma((GC - 1,)), dma((GC - 1,)), dma((3,)),
        ],
        compiler_params=pltpu.CompilerParams(
            collective_id=1, has_side_effects=True, vmem_limit_bytes=60 * 1024 * 1024),
        name="grid_rows",
    )(rows, asked, take)


def local(gaussian, left_basis, right_basis, tile_ranks, diag_factor, morton_of_grid):
    zt = gaussian.T.reshape(2, HALF, NK * CHUNK)
    morton = morton_of_grid.reshape(PTS // 128, 128)
    rows, asked, take = sums_call(zt, left_basis, right_basis, tile_ranks, diag_factor, morton)
    return grid_call(rows, asked.reshape(GC * 1024), take.reshape(PTS)).T


def solution(mesh):
    placed = (
        P("trow", "tcol"),
        P("tcol", "trow", None, None),
        P("tcol", "trow", None, None),
        P("tcol", "trow"),
        P("tcol", "trow", None),
        P("tcol"),
    )
    return jax.shard_map(
        local, mesh=mesh, in_specs=placed, out_specs=P("tcol", "trow"), check_vma=False
    )
```
